128 devices in a mesh: tm: 8 (over z_hi, x), chan: 16 (over y, z_lo, core).
Axes of the slice: x: 4, y: 4, z: 4 (z_hi: 2, z_lo: 2; z = z_hi * 2 + z_lo), core: 2. Of those that a mesh axis runs over, the one named last changes fastest.
Arguments:
- strain: float32 [1024, 65536], P('chan', 'tm'), may hold values from -6 to 6
- fir_taps: float32 [64], replicated, may hold values from -0.75 to 0.75
- source_index: int32 [64], replicated, may hold values from 0 to 1023, as said below
Outputs:
- correlation: float32 [1024, 64, 512], P(('chan', 'tm'))
The draws below stay inside these ranges and needn't reach their ends.
Inputs may be any that keep to these rules, and one draw needn't show every extreme that they name: `source_index`: point numbers; both 0 and 1023 occur, others may repeat.
All inputs are finite; a program needn't handle non-finite values.
Results may differ from the reference program's by a relative error of at most 0.0003.
Values sent between devices are 32-bit elements; how exact they have to be, the bound alone decides.
A program may use at most 128 MiB of HBM per device.

```python
import jax
import jax.numpy as jnp
from jax import lax

P_SIZE = 128
Q = 128
TAPS = 64
NSRC = 64
LAG_ROWS = 4
NT = 16384
SAMPLES = 65536
CHANNELS = 1024


def draw_source_index(key, part):
    key = jax.random.fold_in(key, 7)
    first, second = jax.random.split(key)
    picks = jax.random.randint(first, (NSRC,), 0, CHANNELS, dtype=jnp.int32)
    places = jax.random.permutation(second, NSRC)
    picks = picks.at[places[0]].set(0)
    picks = picks.at[places[1]].set(CHANNELS - 1)
    return picks


def levels(own_key, extent, shards, low, largest):
    level = 1.0
    for dim, parts in shards:
        heights = jax.random.uniform(jax.random.fold_in(jax.random.fold_in(own_key, 6), dim), (parts,), jnp.float32, low / len(shards), largest / len(shards))
        level = level * jnp.repeat(jnp.exp(heights), extent[dim] // parts).reshape((-1,) + (1,) * (len(extent) - 1 - dim))
    return level


def bell_draw(stream_key, shape, deviation, most, cuts=(), kind=jnp.bfloat16):
    array = deviation * jax.random.normal(stream_key, shape, jnp.float32)
    if cuts:
        array = array * levels(stream_key, shape, cuts, -0.22, 0.18)
    return jnp.clip(array, -most, most).astype(kind)


def setup_inputs(seed: int = 0) -> dict:
    keys = jax.random.split(jax.random.key(seed), 4)
    return {
        "strain": bell_draw(keys[0], (CHANNELS, SAMPLES), 1.0, 6.0, ((0, 16), (1, 8)), jnp.float32),
        "fir_taps": bell_draw(keys[1], (TAPS,), TAPS ** -0.5, 0.75, (), jnp.float32),
        "source_index": draw_source_index(jax.random.fold_in(keys[3], 71), 0),
    }


white_floor = 0.1

def tables(size_a, size_b, total):
    first = jnp.arange(size_a, dtype=jnp.int32)
    second = jnp.arange(size_b, dtype=jnp.int32)
    phase = (first[:, None] * second[None, :] % total).astype(jnp.float32)
    angle = 2.0 * jnp.pi / total * phase
    return (jnp.cos(angle), jnp.sin(angle))

def lag_tables():
    rows = (jnp.arange(LAG_ROWS, dtype=jnp.int32) + Q - LAG_ROWS // 2) % Q
    cols = jnp.arange(Q, dtype=jnp.int32)
    phase = (rows[:, None] * cols[None, :] % Q).astype(jnp.float32)
    angle = 2.0 * jnp.pi / Q * phase
    return (jnp.cos(angle), jnp.sin(angle))

def forward(series):
    high = lax.Precision.HIGHEST
    cos_q, sin_q = tables(Q, Q, Q)
    part_re = jnp.einsum('kq,bqp->bkp', cos_q, series, precision=high)
    part_im = -jnp.einsum('kq,bqp->bkp', sin_q, series, precision=high)
    cos_t, sin_t = tables(Q, P_SIZE, NT)
    turn_re = part_re * cos_t + part_im * sin_t
    turn_im = part_im * cos_t - part_re * sin_t
    cos_p, sin_p = tables(P_SIZE, P_SIZE, P_SIZE)
    spec_re = jnp.einsum('bkm,mn->bkn', turn_re, cos_p, precision=high) + jnp.einsum('bkm,mn->bkn', turn_im, sin_p, precision=high)
    spec_im = jnp.einsum('bkm,mn->bkn', turn_im, cos_p, precision=high) - jnp.einsum('bkm,mn->bkn', turn_re, sin_p, precision=high)
    return (spec_re, spec_im)

def whiten(spec_re, spec_im):
    energy = spec_re * spec_re + spec_im * spec_im
    power = lax.optimization_barrier(jnp.mean(energy, axis=(1, 2), keepdims=True))
    denom = jnp.sqrt(energy + white_floor * power)
    return (spec_re / denom, spec_im / denom)

def correlate(chan_re, chan_im, src_re, src_im):
    high = lax.Precision.HIGHEST
    prod_re = src_re * chan_re + src_im * chan_im
    prod_im = src_re * chan_im - src_im * chan_re
    cos_p, sin_p = tables(P_SIZE, P_SIZE, P_SIZE)
    back_re = jnp.einsum('skn,nm->skm', prod_re, cos_p, precision=high) - jnp.einsum('skn,nm->skm', prod_im, sin_p, precision=high)
    back_im = jnp.einsum('skn,nm->skm', prod_im, cos_p, precision=high) + jnp.einsum('skn,nm->skm', prod_re, sin_p, precision=high)
    cos_t, sin_t = tables(Q, P_SIZE, NT)
    turn_re = back_re * cos_t - back_im * sin_t
    turn_im = back_im * cos_t + back_re * sin_t
    cos_l, sin_l = lag_tables()
    lagged = jnp.einsum('rk,skm->srm', cos_l, turn_re, precision=high) - jnp.einsum('rk,skm->srm', sin_l, turn_im, precision=high)
    return lagged.reshape(lagged.shape[0], LAG_ROWS * P_SIZE) * (1.0 / jnp.sqrt(jnp.float32(NT)))

def filter_blocks(padded, fir_taps, count):
    blocks = TAPS // 4
    matrix = fir_taps.reshape(blocks, 4)[:, ::-1]
    total = jnp.zeros((padded.shape[0], count), jnp.float32)
    for offset in range(blocks):
        start = blocks - 1 - offset
        total = total + lax.optimization_barrier(jnp.sum(padded[:, start:start + count, :] * matrix[offset], axis=-1))
    return total

def reference(strain, fir_taps, source_index):
    channels = strain.shape[0]
    blocked = strain.reshape(channels, NT, 4)
    padded = jnp.pad(blocked, ((0, 0), (TAPS // 4 - 1, 0), (0, 0)))
    decimated = filter_blocks(padded, fir_taps, NT)
    spec_re, spec_im = forward(decimated.reshape(channels, Q, P_SIZE))
    white_re, white_im = whiten(spec_re, spec_im)
    src_re = white_re[source_index]
    src_im = white_im[source_index]

    def one_channel(pair):
        return correlate(pair[0], pair[1], src_re, src_im)
    return lax.map(one_channel, (white_re, white_im))
```

```python
import functools

import jax
import jax.numpy as jnp
import ml_dtypes
import numpy as np
from jax import lax
from jax.experimental import pallas as pl
from jax.experimental.pallas import tpu as pltpu
from jax.sharding import PartitionSpec as P

MESH = pl.DeviceIdType.MESH
VMEM = pltpu.VMEM
N = 128
NT = N * N
HALF = N // 2
TAPS = 64
NSRC = 64
FLOOR = 0.1
LAG_ROWS = 4
GROUP = 64
TM = 8
BLOCKS = 16
SPILL = BLOCKS
BAND = 5 * N
RS = BLOCKS // 2 + 1
KINDS = ((0, 24, "xyz"), (24, 24, "yzx"), (48, 16, "zxy"))
VMEM_LIMIT = 56 * 1024 * 1024


def split_np(table):
    high = table.astype(np.float32).astype(ml_dtypes.bfloat16)
    low = (table - high.astype(np.float64)).astype(np.float32).astype(ml_dtypes.bfloat16)
    return high, low


def stack_np(table):
    return np.stack(split_np(table))


def series_tables():
    k = np.arange(HALF)[:, None]
    q = np.arange(N)[None, :]
    ang = 2 * np.pi * ((k * q) % N) / N
    first = np.concatenate([np.cos(ang), -np.sin(ang)])
    first[HALF] = np.cos(np.pi * np.arange(N))
    ang = 2 * np.pi * ((np.arange(N)[:, None] * np.arange(N)[None, :]) % N) / N
    c, s = np.cos(ang), np.sin(ang)
    second = np.block([[c, -s], [s, c]])
    third = np.block([[c, s], [-s, c]])
    ang = 2 * np.pi * ((np.arange(N)[:, None] * np.arange(HALF)[None, :]) % N) / N
    last = np.concatenate([2 * np.cos(ang), -2 * np.sin(ang)], axis=1) / N
    last[:, 0] = 1.0 / N
    last[:, HALF] = np.cos(np.pi * np.arange(N)) / N
    ang = 2 * np.pi * (np.arange(HALF + 8)[:, None] * np.arange(N)[None, :]) / NT
    turn = np.stack([np.cos(ang), np.sin(ang)]).astype(np.float32)
    return first, second, third, last, turn


def window_tables():
    f = np.arange(N)[:, None]
    u = np.arange(2 * N)[None, :]
    ang = 2 * np.pi * ((f * u) % (2 * N)) / (2 * N)
    win = np.concatenate([np.cos(ang), -np.sin(ang)])
    win[N] = np.cos(np.pi * np.arange(2 * N))
    m = np.arange(N)[None, :]
    ang = 2 * np.pi * ((f * m) % (2 * N)) / (2 * N)
    scale = 1.0 / (2 * N * N)
    back = np.concatenate([2 * np.cos(ang), -2 * np.sin(ang)]) * scale
    back[0] = scale
    back[N] = np.cos(np.pi * np.arange(N)) * scale
    return win, back


def split(value):
    high = value.astype(jnp.bfloat16)
    low = (value - high.astype(jnp.float32)).astype(jnp.bfloat16)
    return high, low


def mm(a, b):
    return jnp.dot(a, b, preferred_element_type=jnp.float32)


def mm3(a, b):
    return mm(a[0], b[0]) + mm(a[0], b[1]) + mm(a[1], b[0])


def filter_kernel(strain_ref, taps_ref, index_ref, dec_ref, src_ref, band):
    rho = lax.broadcasted_iota(jnp.int32, (8, N), 0)
    lane = lax.broadcasted_iota(jnp.int32, (8, N), 1)
    shifted = 4 * lane - rho
    base = jnp.zeros((8, N), jnp.float32)
    for j in range(TAPS):
        base = base + jnp.where(shifted == j - 3, taps_ref[j], 0.0)
    base = jnp.where(shifted >= -3, base, 0.0)
    for t in range(BAND // 8):
        move = 2 * t - 32
        tap = 4 * lane + (131 - 8 * t) - rho
        rolled = base if move % N == 0 else pltpu.roll(base, move % N, 1)
        rows = jnp.where((tap >= 0) & (tap < TAPS), rolled, 0.0)
        band[8 * t : 8 * t + 8, :] = rows
    b_hi, b_lo = split(band[...])
    both = jnp.concatenate([b_hi, b_lo], axis=1)

    base_channel = lax.axis_index("chan") * GROUP
    owned = lax.broadcasted_iota(jnp.int32, (NSRC, 2 * GROUP), 1) % GROUP + base_channel
    picker = jnp.where(index_ref[...] == owned, 1.0, 0.0).astype(jnp.bfloat16)

    def finish(block, out):
        for j in range(TM):
            dec_ref[j, block] = out[8 * j : 8 * j + 8]
        picked = mm(picker, jnp.concatenate(split(out), axis=0))
        for j in range(NSRC // 8):
            src_ref[j, block] = picked[8 * j : 8 * j + 8]

    step = 4
    for b0 in range(0, BLOCKS, step):
        his, los = [], []
        for b in range(b0, b0 + step):
            if b == 0:
                x = jnp.concatenate([jnp.zeros((GROUP, N), jnp.float32), strain_ref[:, : 4 * N]], axis=1)
            else:
                x = strain_ref[:, 4 * N * b - N : 4 * N * (b + 1)]
            hi, lo = split(x)
            his.append(hi)
            los.append(lo)
        hi = jnp.concatenate(his, axis=0)
        lo = jnp.concatenate(los, axis=0)
        wide = mm(hi, both)
        out = wide[:, :N] + wide[:, N:] + mm(lo, b_hi)
        for b in range(b0, b0 + step):
            finish(b, out[GROUP * (b - b0) : GROUP * (b - b0 + 1)])
    hi, lo = split(strain_ref[:, 4 * N * BLOCKS - N :])
    wide = mm(hi, both[:N])
    finish(SPILL, wide[:, :N] + wide[:, N:] + mm(lo, b_hi[:N]))


def run_filter(strain, fir_taps, source_index):
    return pl.pallas_call(
        filter_kernel,
        out_shape=[jax.ShapeDtypeStruct((8, BLOCKS + 1, 8, N), jnp.float32)] * 2,
        in_specs=[
            pl.BlockSpec(memory_space=VMEM),
            pl.BlockSpec(memory_space=pltpu.SMEM),
            pl.BlockSpec(memory_space=VMEM),
        ],
        out_specs=[pl.BlockSpec(memory_space=VMEM)] * 2,
        scratch_shapes=[VMEM((BAND, N), jnp.float32)],
        compiler_params=pltpu.CompilerParams(vmem_limit_bytes=VMEM_LIMIT),
        name="decimate",
    )(strain, fir_taps, source_index.reshape(NSRC, 1))


def exchange_kernel(dec_ref, src_ref, chan_out, rows_out, rs_buf, acc, row_buf, d_send, d_recv, s_send, s_recv, r_send, r_recv, own_sem):
    tm = lax.axis_index("tm")
    ch = lax.axis_index("chan")
    pair = ch // 2
    core = ch % 2
    peers = [((tm + d) % TM, ch) for d in range(1, TM)]
    peers += [(tm, (ch + d) % 16) for d in range(1, 16)]
    peers += [((tm + d) % TM, 2 * pair + 1 - core) for d in range(1, TM)]
    barrier = pltpu.get_barrier_semaphore()
    for peer in peers:
        pl.semaphore_signal(barrier, inc=1, device_id=peer, device_id_type=MESH)
    pl.semaphore_wait(barrier, len(peers))

    copies = []
    picks = []
    for d in range(1, 16):
        other = (ch + d) % 16
        copy = pltpu.make_async_remote_copy(
            src_ref=src_ref.at[other // 2, pl.ds((other % 2) * (RS - 1), RS)],
            dst_ref=rs_buf.at[d],
            send_sem=s_send.at[d],
            recv_sem=s_recv.at[d],
            device_id=(tm, other),
            device_id_type=MESH,
        )
        copy.start()
        picks.append(copy)
    for d in range(1, TM):
        other = (tm + d) % TM
        copy = pltpu.make_async_remote_copy(
            src_ref=dec_ref.at[other],
            dst_ref=chan_out.at[tm],
            send_sem=d_send.at[d],
            recv_sem=d_recv.at[d],
            device_id=(other, ch),
            device_id_type=MESH,
        )
        copy.start()
        copies.append(copy)
    own = pltpu.make_async_copy(dec_ref.at[tm], chan_out.at[tm], own_sem.at[0])
    own.start()
    for copy in picks:
        copy.wait_recv()
    total = src_ref[pair, pl.ds(core * (RS - 1), RS)]
    for d in range(1, 16):
        total = total + rs_buf[d]
    acc[...] = total.reshape(RS * 8, N)
    for j in range(TM):
        row_buf[j, :RS] = acc[pl.ds(j, RS, stride=8), :]
        row_buf[j, RS:] = jnp.zeros((16 - RS, N), jnp.float32)
    rows = []
    for d in range(TM):
        for e in range(2):
            if d == 0 and e == 0:
                continue
            other = (tm + d) % TM
            copy = pltpu.make_async_remote_copy(
                src_ref=row_buf.at[other],
                dst_ref=rows_out.at[core, tm],
                send_sem=r_send.at[d, e],
                recv_sem=r_recv.at[d, e],
                device_id=(other, 2 * pair + (core + e) % 2),
                device_id_type=MESH,
            )
            copy.start()
            rows.append(copy)
    mine = pltpu.make_async_copy(row_buf.at[tm], rows_out.at[core, tm], own_sem.at[1])
    mine.start()
    for copy in picks:
        copy.wait_send()
    for copy in copies + rows:
        copy.wait()
    own.wait()
    mine.wait()


def run_exchange(dec, src):
    dma = pltpu.SemaphoreType.DMA
    return pl.pallas_call(
        exchange_kernel,
        out_shape=[
            jax.ShapeDtypeStruct((TM, BLOCKS + 1, 8, N), jnp.float32),
            jax.ShapeDtypeStruct((2, TM, 16, N), jnp.float32),
        ],
        in_specs=[pl.BlockSpec(memory_space=VMEM)] * 2,
        out_specs=[pl.BlockSpec(memory_space=VMEM)] * 2,
        scratch_shapes=[
            VMEM((16, RS, 8, N), jnp.float32),
            VMEM((RS * 8, N), jnp.float32),
            VMEM((TM, 16, N), jnp.float32),
            dma((TM,)),
            dma((TM,)),
            dma((16,)),
            dma((16,)),
            dma((TM, 2)),
            dma((TM, 2)),
            dma((2,)),
        ],
        compiler_params=pltpu.CompilerParams(collective_id=0, has_side_effects=True, vmem_limit_bytes=VMEM_LIMIT),
        name="exchange",
    )(dec, src)


def whiten_series(series, first, second, third, last, turn):
    count = len(series)
    powers = [jnp.sum(x * x) for x in series]
    x_hi, x_lo = split(jnp.concatenate(series, axis=1))
    a_hi, a_lo = first[0], first[1]
    part = mm(jnp.concatenate([a_hi, a_hi], axis=1), jnp.concatenate([x_hi, x_lo], axis=0)) + mm(a_lo, x_hi)
    cos, sin = turn[0, :HALF], turn[1, :HALF]
    cos_mid, sin_mid = turn[0, HALF : HALF + 1], turn[1, HALF : HALF + 1]
    top = lax.broadcasted_iota(jnp.int32, (HALF, N), 0) == 0
    cos_im = jnp.where(top, 0.0, cos)
    rows, mids = [], []
    for i in range(count):
        re = part[:HALF, N * i : N * (i + 1)]
        im = part[HALF:, N * i : N * (i + 1)]
        rows.append(jnp.concatenate([re * cos + im * sin, im * cos_im - re * sin], axis=1))
        mid = im[:1]
        mids.append(jnp.concatenate([mid * cos_mid, -mid * sin_mid], axis=1))
    pad = -count % 8
    if pad:
        mids.append(jnp.zeros((pad, 2 * N), jnp.float32))
    turned = jnp.concatenate(rows + mids, axis=0)
    spec = mm3(split(turned), (second[0], second[1]))
    spec_re, spec_im = spec[:, :N], spec[:, N:]
    energy = spec_re * spec_re + spec_im * spec_im
    floor = [jnp.broadcast_to(FLOOR * p, (HALF, N)) for p in powers]
    floor += [jnp.broadcast_to(FLOOR * p, (1, N)) for p in powers]
    if pad:
        floor.append(jnp.ones((pad, N), jnp.float32))
    scale = lax.rsqrt(energy + jnp.concatenate(floor, axis=0))
    white = jnp.concatenate([spec_re * scale, spec_im * scale], axis=1)
    back = mm3(split(white), (third[0], third[1]))
    cols = []
    for i in range(count):
        re = back[HALF * i : HALF * (i + 1), :N]
        im = back[HALF * i : HALF * (i + 1), N:]
        mid = HALF * count + i
        mid_re, mid_im = back[mid : mid + 1, :N], back[mid : mid + 1, N:]
        out_re = re * cos - im * sin
        out_im = jnp.where(top, mid_re * cos_mid - mid_im * sin_mid, im * cos + re * sin)
        cols.append(jnp.concatenate([out_re, out_im], axis=0))
    y_hi, y_lo = split(jnp.concatenate(cols, axis=1))
    l_hi, l_lo = last[0], last[1]
    time = mm(jnp.concatenate([l_hi, l_hi], axis=1), jnp.concatenate([y_hi, y_lo], axis=0)) + mm(l_lo, y_hi)
    return [time[:, N * i : N * (i + 1)].T for i in range(count)]


def whiten_kernel(chan_ref, rows_ref, first, second, third, last, turn, win, src_out, chan_out, flat, spec):
    series = []
    flat[...] = chan_ref[:, :BLOCKS].reshape(TM * BLOCKS * 8, N)
    place = lax.broadcasted_iota(jnp.int32, (N, N), 0)
    for c in range(8):
        x = flat[pl.ds(c, N, stride=8), :]
        extra = [jnp.zeros((BLOCKS, N), jnp.float32)]
        for j in range(TM - 1):
            tail = chan_ref[j, SPILL, c : c + 1, :]
            extra.append(jnp.broadcast_to(tail, (BLOCKS, N)))
        extra = jnp.concatenate(extra, axis=0)
        series.append(x + jnp.where(place % BLOCKS == 0, extra, 0.0))
    pieces = []
    for j in range(TM):
        early = rows_ref[0, j, : RS - 1]
        if j > 0:
            tail = rows_ref[1, j - 1, RS - 1 : RS]
            early = early + jnp.where(place[: RS - 1] == 0, tail, 0.0)
        pieces += [early, rows_ref[1, j, : RS - 1]]
    series.append(jnp.concatenate(pieces, axis=0))
    whites = whiten_series(series, first, second, third, last, turn)
    src_out[...] = whites[8]
    data = [jnp.concatenate([w, pltpu.roll(w, N - 1, 1)], axis=0) for w in whites[:8]]
    res = mm3((win[0], win[1]), split(jnp.concatenate(data, axis=1)))
    for i in range(2 * N // 8):
        for c in range(8):
            spec[i, 8 * c : 8 * c + 8] = res[8 * i : 8 * i + 8, N * c : N * (c + 1)]

    def slots(i, carry):
        for k in range(8):
            re = spec[i, pl.ds(k, 8, stride=8), :]
            im = spec[i + N // 8, pl.ds(k, 8, stride=8), :]
            if k == 0:
                single = jnp.broadcast_to(i == 0, re.shape)
                res_re = (re, jnp.where(single, 0.0, im))
                res_im = (jnp.where(single, 0.0, im), jnp.where(single, im, -re))
            else:
                res_re = (re, im)
                res_im = (im, -re)
            whole = []
            for halves in (res_re, res_im):
                for r in range(-LAG_ROWS // 2, LAG_ROWS // 2):
                    moved = [h if r == 0 else pltpu.roll(h, -r % N, 1) for h in halves]
                    whole.append(jnp.concatenate(moved, axis=1))
            hi, lo = split(jnp.concatenate(whole, axis=0))
            chan_out[i * 8 + k] = jnp.concatenate([hi, lo], axis=0)
        return carry

    lax.fori_loop(0, N // 8, slots, 0)


def run_whiten(chan, rows, tables):
    return pl.pallas_call(
        whiten_kernel,
        out_shape=[
            jax.ShapeDtypeStruct((N, N), jnp.float32),
            jax.ShapeDtypeStruct((N, N, 2 * N), jnp.bfloat16),
        ],
        in_specs=[pl.BlockSpec(memory_space=VMEM)] * 8,
        out_specs=[pl.BlockSpec(memory_space=VMEM)] * 2,
        scratch_shapes=[VMEM((TM * BLOCKS * 8, N), jnp.float32), VMEM((2 * N // 8, 64, N), jnp.float32)],
        compiler_params=pltpu.CompilerParams(vmem_limit_bytes=VMEM_LIMIT),
        name="whiten",
    )(chan, rows, *tables)


def gather_kernel(own_ref, out, own_sem, send, recv, f_send, f_recv):
    tm = lax.axis_index("tm")
    ch = lax.axis_index("chan")
    x, zh = tm % 4, tm // 4
    y, zl, core = ch // 4, (ch // 2) % 2, ch % 2
    z = 2 * zh + zl

    def device(axis, d):
        if axis == "x":
            return (zh * 4 + (x + d) % 4, ch)
        if axis == "y":
            return (tm, ((y + d) % 4) * 4 + zl * 2 + core)
        other = (z + d) % 4
        return ((other // 2) * 4 + x, y * 4 + (other % 2) * 2 + core)

    sibling = (tm, ch + 1 - 2 * core)
    peers = [device(axis, d) for axis in "xyz" for d in (1, 2, 3)] + [sibling]
    barrier = pltpu.get_barrier_semaphore()
    for peer in peers:
        pl.semaphore_signal(barrier, inc=1, device_id=peer, device_id_type=MESH)

    mine = pltpu.make_async_copy(own_ref, out.at[y, zl, zh, x], own_sem)
    mine.start()
    mine.wait()
    pl.semaphore_wait(barrier, len(peers))

    def region(kind, phase, d=0):
        start, size, order = KINDS[kind]
        at = {"x": x, "y": y, "z": z}
        axis = order[phase]
        at[axis] = (at[axis] - d) % 4
        done = order[:phase]
        whole = slice(None)
        ix = whole if "x" in done else at["x"]
        iy = whole if "y" in done else at["y"]
        il = whole if "z" in done else at["z"] % 2
        ih = whole if "z" in done else at["z"] // 2
        return out.at[iy, il, ih, ix, pl.ds(core * HALF + start, size)]

    started = []
    for phase in range(3):
        for kind in range(3):
            axis = KINDS[kind][2][phase]
            part = region(kind, phase)
            for d in (1, 3, 2):
                copy = pltpu.make_async_remote_copy(
                    src_ref=part,
                    dst_ref=part,
                    send_sem=send.at[kind, phase, d],
                    recv_sem=recv.at[kind, phase, d],
                    device_id=device(axis, d),
                    device_id_type=MESH,
                )
                copy.start()
                started.append(copy)
        for kind in range(3):
            axis = KINDS[kind][2][phase]
            for d in (1, 3, 2):
                came = region(kind, phase, d)
                pltpu.make_async_remote_copy(
                    src_ref=came,
                    dst_ref=came,
                    send_sem=send.at[kind, phase, d],
                    recv_sem=recv.at[kind, phase, d],
                    device_id=sibling,
                    device_id_type=MESH,
                ).wait_recv()
                copy = pltpu.make_async_remote_copy(
                    src_ref=came,
                    dst_ref=came,
                    send_sem=f_send.at[kind, phase, d],
                    recv_sem=f_recv.at[kind, phase, d],
                    device_id=sibling,
                    device_id_type=MESH,
                )
                copy.start()
                started.append((copy,))
    for copy in started:
        if isinstance(copy, tuple):
            copy[0].wait()
        else:
            copy.wait_send()


def run_gather(own):
    dma = pltpu.SemaphoreType.DMA
    return pl.pallas_call(
        gather_kernel,
        out_shape=jax.ShapeDtypeStruct((4, 2, 2, 4, N, N), jnp.float32),
        in_specs=[pl.BlockSpec(memory_space=VMEM)],
        out_specs=pl.BlockSpec(memory_space=VMEM),
        scratch_shapes=[pltpu.SemaphoreType.DMA] + [dma((3, 3, 4))] * 4,
        compiler_params=pltpu.CompilerParams(collective_id=1, has_side_effects=True, vmem_limit_bytes=VMEM_LIMIT),
        name="gather_sources",
    )(own)


def correlate_kernel(src_ref, chan_ref, win, back, out_ref, spec, prod):
    w_hi, w_lo = win[0][:, :N], win[1][:, :N]
    w_both = jnp.concatenate([w_hi, w_hi], axis=1)

    def transform(g, carry):
        pair = jnp.concatenate([src_ref[2 * g], src_ref[2 * g + 1]], axis=1)
        hi, lo = split(pair)
        res = mm(w_both, jnp.concatenate([hi, lo], axis=0)) + mm(w_lo, hi)
        for i in range(2 * N // 8):
            for e in range(2):
                spec[i, pl.ds(pl.multiple_of((2 * g + e) * 8, 8), 8), :] = res[8 * i : 8 * i + 8, N * e : N * (e + 1)]
        return carry

    lax.fori_loop(0, NSRC // 2, transform, 0)
    left = lax.broadcasted_iota(jnp.int32, (64, N), 1) < HALF

    def slots(i, carry):
        for k in range(8):
            re = spec[i, pl.ds(k, NSRC, stride=8), :]
            im = spec[i + N // 8, pl.ds(k, NSRC, stride=8), :]
            hi, lo = split(jnp.concatenate([re, im], axis=1))
            s_both = jnp.concatenate([hi, lo], axis=0)
            res = lax.dot_general(
                chan_ref[i * 8 + k], s_both, (((1,), (1,)), ((), ())), preferred_element_type=jnp.float32
            )
            u = res[:64] + jnp.where(left, res[64:], 0.0)
            v = u + pltpu.roll(u, HALF, 1)
            prod[pl.ds(pl.multiple_of((i * 8 + k) * 32, 32), 32), :] = jnp.where(left[:32], v[:32], v[32:])
        return carry

    lax.fori_loop(0, N // 8, slots, 0)
    b_hi, b_lo = back[0], back[1]
    for r in range(LAG_ROWS):
        for c in range(8):
            t = prod[pl.ds(r * 8 + c, N, stride=32), :].T
            hi, lo = split(jnp.concatenate([t[:NSRC], t[NSRC:]], axis=1))
            out_ref[c, :, N * r : N * (r + 1)] = mm(hi, b_hi) + mm(hi, b_lo) + mm(lo, b_hi)


def run_correlate(src, chan, win, back):
    return pl.pallas_call(
        correlate_kernel,
        out_shape=jax.ShapeDtypeStruct((8, NSRC, LAG_ROWS * N), jnp.float32),
        in_specs=[pl.BlockSpec(memory_space=VMEM)] * 4,
        out_specs=pl.BlockSpec(memory_space=VMEM),
        scratch_shapes=[VMEM((2 * N // 8, 8 * NSRC, N), jnp.float32), VMEM((N * 32, N), jnp.float32)],
        compiler_params=pltpu.CompilerParams(vmem_limit_bytes=VMEM_LIMIT),
        name="correlate",
    )(src, chan, win, back)


def on_device(strain, fir_taps, source_index):
    first, second, third, last, turn = series_tables()
    win, back = window_tables()
    win = stack_np(win)
    dec, src = run_filter(strain, fir_taps, source_index)
    chan, rows = run_exchange(dec, src)
    own, chan_op = run_whiten(
        chan, rows, (stack_np(first), stack_np(second), stack_np(third), stack_np(last), turn, win)
    )
    sources = run_gather(own).reshape(NSRC, N, N)
    return run_correlate(sources, chan_op, win, stack_np(back))


def solution(mesh):
    return jax.shard_map(
        on_device,
        mesh=mesh,
        in_specs=(P("chan", "tm"), P(), P()),
        out_specs=P(("chan", "tm"), None, None),
        check_vma=False,
    )
```

```python
import functools

import jax
import jax.numpy as jnp
import ml_dtypes
import numpy as np
from jax import lax
from jax.experimental import pallas as pl
from jax.experimental.pallas import tpu as pltpu
from jax.sharding import PartitionSpec as P

MESH = pl.DeviceIdType.MESH
VMEM = pltpu.VMEM
N = 128
NT = N * N
HALF = N // 2
TAPS = 64
NSRC = 64
FLOOR = 0.1
LAG_ROWS = 4
GROUP = 64
TM = 8
BLOCKS = 16
BAND = 5 * N
HB = BLOCKS // 2
PART = HB + 1
KINDS = ((0, 24, "xyz"), (24, 24, "yzx"), (48, 16, "zxy"))
ORDER = (1, 3, 2)
PLANES = (0, 1, 3, 2)
VMEM_LIMIT = 56 * 1024 * 1024


def split_np(table):
    high = table.astype(np.float32).astype(ml_dtypes.bfloat16)
    low = (table - high.astype(np.float64)).astype(np.float32).astype(ml_dtypes.bfloat16)
    return high, low


def stack_np(table):
    return np.stack(split_np(table))


def series_tables():
    k = np.arange(HALF)[:, None]
    q = np.arange(N)[None, :]
    ang = 2 * np.pi * ((k * q) % N) / N
    first = np.concatenate([np.cos(ang), -np.sin(ang)])
    first[HALF] = np.cos(np.pi * np.arange(N))
    ang = 2 * np.pi * ((np.arange(N)[:, None] * np.arange(N)[None, :]) % N) / N
    c, s = np.cos(ang), np.sin(ang)
    second = np.block([[c, -s], [s, c]])
    third = np.block([[c, s], [-s, c]])
    ang = 2 * np.pi * ((np.arange(N)[:, None] * np.arange(HALF)[None, :]) % N) / N
    last = np.concatenate([2 * np.cos(ang), -2 * np.sin(ang)], axis=1) / N
    last[:, 0] = 1.0 / N
    last[:, HALF] = np.cos(np.pi * np.arange(N)) / N
    ang = 2 * np.pi * (np.arange(HALF + 8)[:, None] * np.arange(N)[None, :]) / NT
    turn = np.stack([np.cos(ang), np.sin(ang)]).astype(np.float32)
    return first, second, third, last, turn


def window_tables():
    f = np.arange(N)[:, None]
    u = np.arange(2 * N)[None, :]
    ang = 2 * np.pi * ((f * u) % (2 * N)) / (2 * N)
    win = np.concatenate([np.cos(ang), -np.sin(ang)])
    win[N] = np.cos(np.pi * np.arange(2 * N))
    m = np.arange(N)[None, :]
    ang = 2 * np.pi * ((f * m) % (2 * N)) / (2 * N)
    scale = 1.0 / (2 * N * N)
    back = np.concatenate([2 * np.cos(ang), -2 * np.sin(ang)]) * scale
    back[0] = scale
    back[N] = np.cos(np.pi * np.arange(N)) * scale
    return win, back


def split(value):
    high = value.astype(jnp.bfloat16)
    low = (value - high.astype(jnp.float32)).astype(jnp.bfloat16)
    return high, low


def mm(a, b):
    return jnp.dot(a, b, preferred_element_type=jnp.float32)


def mm3(a, b):
    return mm(a[0], b[0]) + mm(a[0], b[1]) + mm(a[1], b[0])


def whiten_series(series, first, second, third, last, turn):
    count = len(series)
    powers = [jnp.sum(x * x) for x in series]
    x_hi, x_lo = split(jnp.concatenate(series, axis=1))
    a_hi, a_lo = first[0], first[1]
    part = mm(jnp.concatenate([a_hi, a_hi], axis=1), jnp.concatenate([x_hi, x_lo], axis=0)) + mm(a_lo, x_hi)
    cos, sin = turn[0, :HALF], turn[1, :HALF]
    cos_mid, sin_mid = turn[0, HALF : HALF + 1], turn[1, HALF : HALF + 1]
    top = lax.broadcasted_iota(jnp.int32, (HALF, N), 0) == 0
    cos_im = jnp.where(top, 0.0, cos)
    rows, mids = [], []
    for i in range(count):
        re = part[:HALF, N * i : N * (i + 1)]
        im = part[HALF:, N * i : N * (i + 1)]
        rows.append(jnp.concatenate([re * cos + im * sin, im * cos_im - re * sin], axis=1))
        mid = im[:1]
        mids.append(jnp.concatenate([mid * cos_mid, -mid * sin_mid], axis=1))
    pad = -count % 8
    if pad:
        mids.append(jnp.zeros((pad, 2 * N), jnp.float32))
    turned = jnp.concatenate(rows + mids, axis=0)
    spec = mm3(split(turned), (second[0], second[1]))
    spec_re, spec_im = spec[:, :N], spec[:, N:]
    energy = spec_re * spec_re + spec_im * spec_im
    floor = [jnp.broadcast_to(FLOOR * p, (HALF, N)) for p in powers]
    floor += [jnp.broadcast_to(FLOOR * p, (1, N)) for p in powers]
    if pad:
        floor.append(jnp.ones((pad, N), jnp.float32))
    scale = lax.rsqrt(energy + jnp.concatenate(floor, axis=0))
    white = jnp.concatenate([spec_re * scale, spec_im * scale], axis=1)
    back = mm3(split(white), (third[0], third[1]))
    cols = []
    for i in range(count):
        re = back[HALF * i : HALF * (i + 1), :N]
        im = back[HALF * i : HALF * (i + 1), N:]
        mid = HALF * count + i
        mid_re, mid_im = back[mid : mid + 1, :N], back[mid : mid + 1, N:]
        out_re = re * cos - im * sin
        out_im = jnp.where(top, mid_re * cos_mid - mid_im * sin_mid, im * cos + re * sin)
        cols.append(jnp.concatenate([out_re, out_im], axis=0))
    y_hi, y_lo = split(jnp.concatenate(cols, axis=1))
    l_hi, l_lo = last[0], last[1]
    time = mm(jnp.concatenate([l_hi, l_hi], axis=1), jnp.concatenate([y_hi, y_lo], axis=0)) + mm(l_lo, y_hi)
    return [time[:, N * i : N * (i + 1)].T for i in range(count)]


def remote(src, dst, send, recv, device):
    return pltpu.make_async_remote_copy(
        src_ref=src, dst_ref=dst, send_sem=send, recv_sem=recv, device_id=device, device_id_type=MESH
    )


def build_band(taps_ref, band):
    rho = lax.broadcasted_iota(jnp.int32, (8, N), 0)
    lane = lax.broadcasted_iota(jnp.int32, (8, N), 1)
    shifted = 4 * lane - rho
    base = jnp.zeros((8, N), jnp.float32)
    for j in range(TAPS):
        base = jnp.where(shifted == j - 3, taps_ref[j], base)
    for t in range(BAND // 8):
        move = (2 * t - 32) % N
        tap = 4 * lane + (131 - 8 * t) - rho
        rolled = base if move == 0 else pltpu.roll(base, move, 1)
        band[8 * t : 8 * t + 8, :] = jnp.where((tap >= 0) & (tap < TAPS), rolled, 0.0)


def build_picker(index_ref):
    row = lax.broadcasted_iota(jnp.int32, (NSRC, 2 * GROUP), 0)
    wanted = jnp.zeros((NSRC, 2 * GROUP), jnp.int32)
    for s in range(NSRC):
        wanted = jnp.where(row == s, index_ref[s], wanted)
    owned = lax.broadcasted_iota(jnp.int32, (NSRC, 2 * GROUP), 1) % GROUP + lax.axis_index("chan") * GROUP
    return jnp.where(wanted == owned, 1.0, 0.0).astype(jnp.bfloat16)


def kernel(
    strain_hbm, taps_ref, index_ref, first_hbm, second_hbm, third_hbm, last_hbm, turn_hbm, win_hbm, back_hbm, out_ref,
    raw, band, dec, pick, pick_in, total, rs_in, acc, row_buf, rows_in, chan_in, src_all, spec_c, chan_op, spec, prod,
    first, second, third, last, turn, win, back,
    load_sem, own_sem, pick_sem, dec_send, dec_recv, rs_send, rs_recv, row_send, row_recv,
    g_send, g_recv, f_send, f_recv,
):
    tm = lax.axis_index("tm")
    ch = lax.axis_index("chan")
    x, zh = tm % 4, tm // 4
    y, zl, core = ch // 4, (ch // 2) % 2, ch % 2
    z, pair = 2 * zh + zl, ch // 2

    tables = (
        (first_hbm, first), (second_hbm, second), (third_hbm, third), (last_hbm, last), (turn_hbm, turn),
        (win_hbm, win), (back_hbm, back),
    )
    load = pltpu.make_async_copy(strain_hbm, raw.at[:, pl.ds(N, 4 * N * BLOCKS)], load_sem.at[0])
    load.start()
    loads = [pltpu.make_async_copy(a, b, load_sem.at[1 + i]) for i, (a, b) in enumerate(tables)]
    for copy in loads:
        copy.start()

    def device(axis, d):
        if axis == "x":
            return (zh * 4 + (x + d) % 4, ch)
        if axis == "y":
            return (tm, ((y + d) % 4) * 4 + zl * 2 + core)
        other = (z + d) % 4
        return ((other // 2) * 4 + x, y * 4 + (other % 2) * 2 + core)

    sibling = (tm, 2 * pair + 1 - core)
    peers = [sibling]
    peers += [(tm, 2 * ((pair + d) % 8) + core) for d in range(1, 8)]
    peers += [((tm + d) % TM, 2 * pair + (core + e) % 2) for d in range(1, TM) for e in range(2)]
    peers += [((1 - zh) * 4 + x, y * 4 + (1 - zl) * 2 + core)]
    barrier = pltpu.get_barrier_semaphore()
    for peer in peers:
        pl.semaphore_signal(barrier, inc=1, device_id=peer, device_id_type=MESH)

    raw[:, :N] = jnp.zeros((GROUP, N), jnp.float32)
    build_band(taps_ref, band)
    picker = build_picker(index_ref)
    b_hi, b_lo = split(band[...])
    both = jnp.concatenate([b_hi, b_lo], axis=1)
    load.wait()

    def finish(half, block, value):
        for j in range(TM):
            dec[j, half, block] = value[8 * j : 8 * j + 8]
        picked = mm(picker, jnp.concatenate(split(value), axis=0))
        for j in range(NSRC // 8):
            pick[half, j, block] = picked[8 * j : 8 * j + 8]

    hi, lo = split(raw[:, 4 * N * BLOCKS :])
    wide = mm(hi, both[:N])
    finish(1, HB, wide[:, :N] + wide[:, N:] + mm(lo, b_hi[:N]))
    for j in range(TM):
        dec[j, 0, HB] = jnp.zeros((8, N), jnp.float32)
        pick[0, j, HB] = jnp.zeros((8, N), jnp.float32)

    def filter_half(half):
        for b0 in range(0, HB, 4):
            his, los = [], []
            for b in range(b0, b0 + 4):
                start = pl.multiple_of((half * HB + b) * (4 * N), 4 * N)
                hi, lo = split(raw[:, pl.ds(start, BAND)])
                his.append(hi)
                los.append(lo)
            hi, lo = jnp.concatenate(his, axis=0), jnp.concatenate(los, axis=0)
            wide = mm(hi, both)
            value = wide[:, :N] + wide[:, N:] + mm(lo, b_hi)
            for b in range(b0, b0 + 4):
                finish(half, b, value[GROUP * (b - b0) : GROUP * (b - b0 + 1)])

    started = []

    def send_blocks(half, part):
        for d in (1, 3, 2, 4, 5, 7, 6):
            other = (tm + d) % TM
            copy = remote(
                dec.at[other, half], chan_in.at[tm, half], dec_send.at[part, d], dec_recv.at[part, d], (other, ch)
            )
            copy.start()
            started.append(copy)

    filter_half(1 - core)
    pl.semaphore_wait(barrier, len(peers))
    give = remote(pick.at[1 - core], pick_in, pick_sem.at[0], pick_sem.at[1], sibling)
    give.start()
    send_blocks(1 - core, 0)
    filter_half(core)
    own_blocks = pltpu.make_async_copy(dec.at[tm], chan_in.at[tm], own_sem.at[0])
    own_blocks.start()

    give.wait_recv()
    total[...] = pick[core] + pick_in[...]
    sums = []
    for d in (1, 7, 2, 6, 3, 5, 4):
        other = (pair + d) % 8
        copy = remote(total.at[other], rs_in.at[d], rs_send.at[d], rs_recv.at[d], (tm, 2 * other + core))
        copy.start()
        sums.append(copy)
    send_blocks(core, 1)
    for copy in sums:
        copy.wait_recv()
    value = total[pair]
    for d in range(1, 8):
        value = value + rs_in[d]
    acc[...] = value.reshape(PART * 8, N)
    for j in range(TM):
        row_buf[j, :PART] = acc[pl.ds(j, PART, stride=8), :]
        row_buf[j, PART:] = jnp.zeros((16 - PART, N), jnp.float32)
    rows = []
    for d in range(TM):
        for e in range(2):
            if d == 0 and e == 0:
                continue
            other = (tm + d) % TM
            copy = remote(
                row_buf.at[other],
                rows_in.at[core, tm],
                row_send.at[d, e],
                row_recv.at[d, e],
                (other, 2 * pair + (core + e) % 2),
            )
            copy.start()
            rows.append(copy)
    rows_in[core, tm] = row_buf[tm]
    for copy in loads:
        copy.wait()
    for copy in rows:
        copy.wait_recv()
    place = lax.broadcasted_iota(jnp.int32, (HB, N), 0)
    pieces = []
    for j in range(TM):
        early = rows_in[0, j, :HB]
        if j > 0:
            early = early + jnp.where(place == 0, rows_in[1, j - 1, HB : HB + 1], 0.0)
        pieces += [early, rows_in[1, j, :HB]]
    src_all[y, 2 * zl + zh, x] = whiten_series([jnp.concatenate(pieces, axis=0)], first, second, third, last, turn)[0]

    def region(kind, phase, d, plane=None):
        start, size, order = KINDS[kind]
        at = {"x": x, "y": y, "z": z}
        at[order[phase]] = (at[order[phase]] + d) % 4
        done = order[:phase]
        iy = slice(None) if "y" in done else at["y"]
        if plane is not None:
            iy = (y + plane) % 4
        iw = slice(None) if "z" in done else 2 * (at["z"] % 2) + at["z"] // 2
        ix = slice(None) if "x" in done else at["x"]
        return src_all.at[iy, iw, ix, pl.ds(core * HALF + start, size)]

    slots_used = {}

    def slot(*key):
        return slots_used.setdefault(key, len(slots_used))

    def send_part(kind, phase, d, plane=None):
        part = region(kind, phase, 0, plane)
        n = slot(kind, phase, d, plane)
        copy = remote(part, part, g_send.at[n], g_recv.at[n], device(KINDS[kind][2][phase], d))
        copy.start()
        started.append((copy,))

    def pass_on(kind, phase, d, plane=None):
        came = region(kind, phase, -d, plane)
        n = slot(kind, phase, d, plane)
        remote(came, came, g_send.at[n], g_recv.at[n], sibling).wait_recv()
        copy = remote(came, came, f_send.at[n], f_recv.at[n], sibling)
        copy.start()
        started.append((copy,))
        return copy

    for d in ORDER:
        for kind in range(3):
            send_part(kind, 0, d)

    own_blocks.wait()
    for copy in started:
        if not isinstance(copy, tuple):
            copy.wait_recv()

    def channel(c):
        pieces = []
        for j in range(TM):
            for half in range(2):
                value = chan_in[j, half, :HB, c, :]
                if j > 0 and half == 0:
                    value = value + jnp.where(place == 0, chan_in[j - 1, 1, HB, c : c + 1, :], 0.0)
                pieces.append(value)
        return jnp.concatenate(pieces, axis=0)

    def channels(c0):
        whites = whiten_series([channel(c) for c in range(c0, c0 + 4)], first, second, third, last, turn)
        data = [jnp.concatenate([w, pltpu.roll(w, N - 1, 1)], axis=0) for w in whites]
        res = mm3((win[0], win[1]), split(jnp.concatenate(data, axis=1)))
        for i in range(2 * N // 8):
            for c in range(4):
                at = 8 * (c0 + c)
                spec_c[i, at : at + 8] = res[8 * i : 8 * i + 8, N * c : N * (c + 1)]

    channels(0)
    forwards = []
    for d in ORDER:
        for kind in range(3):
            forwards.append(pass_on(kind, 0, d))
    for d in ORDER:
        for kind in range(3):
            send_part(kind, 1, d)
    channels(4)
    for d in ORDER:
        for kind in range(3):
            forwards.append(pass_on(kind, 1, d))
    for d in ORDER:
        send_part(2, 2, d)
        for kind in range(2):
            send_part(kind, 2, d, 0)
    for plane in PLANES[1:]:
        for d in ORDER:
            for kind in range(2):
                send_part(kind, 2, d, plane)

    def channel_slots(i, carry):
        for k in range(8):
            re = spec_c[i, pl.ds(k, 8, stride=8), :]
            im = spec_c[i + N // 8, pl.ds(k, 8, stride=8), :]
            if k == 0:
                single = jnp.broadcast_to(i == 0, re.shape)
                res_re = (re, jnp.where(single, 0.0, im))
                res_im = (jnp.where(single, 0.0, im), jnp.where(single, im, -re))
            else:
                res_re = (re, im)
                res_im = (im, -re)
            whole = []
            for halves in (res_re, res_im):
                for r in range(-LAG_ROWS // 2, LAG_ROWS // 2):
                    moved = [h if r == 0 else pltpu.roll(h, -r % N, 1) for h in halves]
                    whole.append(jnp.concatenate(moved, axis=1))
            hi, lo = split(jnp.concatenate(whole, axis=0))
            chan_op[i * 8 + k] = jnp.concatenate([hi, lo], axis=0)
        return carry

    lax.fori_loop(0, N // 8, channel_slots, 0)

    w_hi, w_lo = win[0][:, :N], win[1][:, :N]
    w_both = jnp.concatenate([w_hi, w_hi], axis=1)

    def transform(at_y):
        def four(g, carry):
            hi, lo = split(jnp.concatenate([src_all[at_y, g, e] for e in range(4)], axis=1))
            res = mm(w_both, jnp.concatenate([hi, lo], axis=0)) + mm(w_lo, hi)
            for i in range(2 * N // 8):
                for e in range(4):
                    at = pl.multiple_of(((at_y * 4 + g) * 4 + e) * 8, 8)
                    spec[i, pl.ds(at, 8), :] = res[8 * i : 8 * i + 8, N * e : N * (e + 1)]
            return carry

        lax.fori_loop(0, 4, four, 0)

    for plane in PLANES:
        if plane:
            forwards.append(pass_on(2, 2, (-plane) % 4))
        for d in ORDER:
            for kind in range(2):
                forwards.append(pass_on(kind, 2, d, plane))
        for copy in forwards:
            copy.wait_recv()
        forwards = []
        transform((y + plane) % 4)

    left = lax.broadcasted_iota(jnp.int32, (64, N), 1) < HALF

    def slots(i, carry):
        for k in range(8):
            re = spec[i, pl.ds(k, NSRC, stride=8), :]
            im = spec[i + N // 8, pl.ds(k, NSRC, stride=8), :]
            hi, lo = split(jnp.concatenate([re, im], axis=1))
            res = lax.dot_general(
                chan_op[i * 8 + k],
                jnp.concatenate([hi, lo], axis=0),
                (((1,), (1,)), ((), ())),
                preferred_element_type=jnp.float32,
            )
            u = res[:64] + jnp.where(left, res[64:], 0.0)
            v = u + pltpu.roll(u, HALF, 1)
            prod[pl.ds(pl.multiple_of((i * 8 + k) * 32, 32), 32), :] = jnp.where(left[:32], v[:32], v[32:])
        return carry

    lax.fori_loop(0, N // 8, slots, 0)
    k_hi, k_lo = back[0], back[1]
    for r in range(LAG_ROWS):
        for c in range(8):
            t = prod[pl.ds(r * 8 + c, N, stride=32), :].T
            hi, lo = split(jnp.concatenate([t[:NSRC], t[NSRC:]], axis=1))
            out_ref[c, :, N * r : N * (r + 1)] = mm(hi, k_hi) + mm(hi, k_lo) + mm(lo, k_hi)

    give.wait_send()
    for copy in sums + rows:
        copy.wait_send()
    for copy in started:
        (copy[0] if isinstance(copy, tuple) else copy).wait_send()


def on_device(strain, fir_taps, source_index):
    tables = series_tables()
    win, back = window_tables()
    tables = [stack_np(t) for t in tables[:4]] + [tables[4], stack_np(win), stack_np(back)]
    dma = pltpu.SemaphoreType.DMA
    f32 = jnp.float32
    smem = pl.BlockSpec(memory_space=pltpu.SMEM)
    anywhere = pl.BlockSpec(memory_space=pl.ANY)
    return pl.pallas_call(
        kernel,
        out_shape=jax.ShapeDtypeStruct((8, NSRC, LAG_ROWS * N), f32),
        in_specs=[anywhere, smem, smem] + [anywhere] * len(tables),
        out_specs=pl.BlockSpec(memory_space=VMEM),
        scratch_shapes=[
            VMEM((GROUP, N + 4 * N * BLOCKS), f32),
            VMEM((BAND, N), f32),
            VMEM((TM, 2, PART, 8, N), f32),
            VMEM((2, 8, PART, 8, N), f32),
            VMEM((8, PART, 8, N), f32),
            VMEM((8, PART, 8, N), f32),
            VMEM((8, PART, 8, N), f32),
            VMEM((PART * 8, N), f32),
            VMEM((TM, 16, N), f32),
            VMEM((2, TM, 16, N), f32),
            VMEM((TM, 2, PART, 8, N), f32),
            VMEM((4, 4, 4, N, N), f32),
            VMEM((2 * N // 8, 64, N), f32),
            VMEM((N, N, 2 * N), jnp.bfloat16),
            VMEM((2 * N // 8, 8 * NSRC, N), f32),
            VMEM((N * 32, N), f32),
        ]
        + [VMEM(t.shape, jnp.dtype(t.dtype)) for t in tables]
        + [
            dma((1 + len(tables),)),
            dma((1,)),
            dma((2,)),
            dma((2, TM)),
            dma((2, TM)),
            dma((8,)),
            dma((8,)),
            dma((TM, 2)),
            dma((TM, 2)),
        ]
        + [dma((48,))] * 4,
        compiler_params=pltpu.CompilerParams(
            collective_id=0, has_side_effects=True, vmem_limit_bytes=VMEM_LIMIT
        ),
        name="interferometry",
    )(strain, fir_taps, source_index, *tables)


def solution(mesh):
    return jax.shard_map(
        on_device,
        mesh=mesh,
        in_specs=(P("chan", "tm"), P(), P()),
        out_specs=P(("chan", "tm"), None, None),
        check_vma=False,
    )
```

```python
import functools

import jax
import jax.numpy as jnp
import ml_dtypes
import numpy as np
from jax import lax
from jax.experimental import pallas as pl
from jax.experimental.pallas import tpu as pltpu
from jax.sharding import PartitionSpec as P

MESH = pl.DeviceIdType.MESH
VMEM = pltpu.VMEM
N = 128
NT = N * N
HALF = N // 2
TAPS = 64
NSRC = 64
FLOOR = 0.1
LAG_ROWS = 4
GROUP = 64
TM = 8
BLOCKS = 16
BAND = 5 * N
HB = BLOCKS // 2
PART = HB + 1
KINDS = ((0, 24, "xyz"), (24, 24, "yzx"), (48, 16, "zxy"))
ORDER = (1, 3, 2)
UNROLL = 32
VMEM_LIMIT = 56 * 1024 * 1024


def split_np(table):
    high = table.astype(np.float32).astype(ml_dtypes.bfloat16)
    low = (table - high.astype(np.float64)).astype(np.float32).astype(ml_dtypes.bfloat16)
    return high, low


def stack_np(table):
    return np.stack(split_np(table))


def series_tables():
    k = np.arange(HALF)[:, None]
    q = np.arange(N)[None, :]
    ang = 2 * np.pi * ((k * q) % N) / N
    first = np.concatenate([np.cos(ang), -np.sin(ang)])
    first[HALF] = np.cos(np.pi * np.arange(N))
    ang = 2 * np.pi * ((np.arange(N)[:, None] * np.arange(N)[None, :]) % N) / N
    c, s = np.cos(ang), np.sin(ang)
    second = np.block([[c, -s], [s, c]])
    third = np.block([[c, s], [-s, c]])
    ang = 2 * np.pi * ((np.arange(N)[:, None] * np.arange(HALF)[None, :]) % N) / N
    last = np.concatenate([2 * np.cos(ang), -2 * np.sin(ang)], axis=1) / N
    last[:, 0] = 1.0 / N
    last[:, HALF] = np.cos(np.pi * np.arange(N)) / N
    ang = 2 * np.pi * (np.arange(HALF + 8)[:, None] * np.arange(N)[None, :]) / NT
    turn = np.stack([np.cos(ang), np.sin(ang)]).astype(np.float32)
    return first, second, third, last, turn


def window_tables():
    f = np.arange(N)[:, None]
    u = np.arange(2 * N)[None, :]
    ang = 2 * np.pi * ((f * u) % (2 * N)) / (2 * N)
    win = np.concatenate([np.cos(ang), -np.sin(ang)])
    win[N] = np.cos(np.pi * np.arange(2 * N))
    m = np.arange(N)[None, :]
    ang = 2 * np.pi * ((f * m) % (2 * N)) / (2 * N)
    scale = 1.0 / (2 * N * N)
    back = np.concatenate([2 * np.cos(ang), -2 * np.sin(ang)]) * scale
    back[0] = scale
    back[N] = np.cos(np.pi * np.arange(N)) * scale
    return win, back


def split(value):
    high = value.astype(jnp.bfloat16)
    low = (value - high.astype(jnp.float32)).astype(jnp.bfloat16)
    return high, low


def mm(a, b):
    return jnp.dot(a, b, preferred_element_type=jnp.float32)


def mm3(a, b):
    return mm(a[0], b[0]) + mm(a[0], b[1]) + mm(a[1], b[0])


def whiten_series(series, first, second, third, last, turn):
    count = len(series)
    powers = [jnp.sum(x * x) for x in series]
    x_hi, x_lo = split(jnp.concatenate(series, axis=1))
    a_hi, a_lo = first[0], first[1]
    part = mm(jnp.concatenate([a_hi, a_hi], axis=1), jnp.concatenate([x_hi, x_lo], axis=0)) + mm(a_lo, x_hi)
    cos, sin = turn[0, :HALF], turn[1, :HALF]
    cos_mid, sin_mid = turn[0, HALF : HALF + 1], turn[1, HALF : HALF + 1]
    top = lax.broadcasted_iota(jnp.int32, (HALF, N), 0) == 0
    cos_im = jnp.where(top, 0.0, cos)
    rows, mids = [], []
    for i in range(count):
        re = part[:HALF, N * i : N * (i + 1)]
        im = part[HALF:, N * i : N * (i + 1)]
        rows.append(jnp.concatenate([re * cos + im * sin, im * cos_im - re * sin], axis=1))
        mid = im[:1]
        mids.append(jnp.concatenate([mid * cos_mid, -mid * sin_mid], axis=1))
    pad = -count % 8
    if pad:
        mids.append(jnp.zeros((pad, 2 * N), jnp.float32))
    turned = jnp.concatenate(rows + mids, axis=0)
    spec = mm3(split(turned), (second[0], second[1]))
    spec_re, spec_im = spec[:, :N], spec[:, N:]
    energy = spec_re * spec_re + spec_im * spec_im
    floor = [jnp.broadcast_to(FLOOR * p, (HALF, N)) for p in powers]
    floor += [jnp.broadcast_to(FLOOR * p, (1, N)) for p in powers]
    if pad:
        floor.append(jnp.ones((pad, N), jnp.float32))
    scale = lax.rsqrt(energy + jnp.concatenate(floor, axis=0))
    white = jnp.concatenate([spec_re * scale, spec_im * scale], axis=1)
    back = mm3(split(white), (third[0], third[1]))
    cols = []
    for i in range(count):
        re = back[HALF * i : HALF * (i + 1), :N]
        im = back[HALF * i : HALF * (i + 1), N:]
        mid = HALF * count + i
        mid_re, mid_im = back[mid : mid + 1, :N], back[mid : mid + 1, N:]
        out_re = re * cos - im * sin
        out_im = jnp.where(top, mid_re * cos_mid - mid_im * sin_mid, im * cos + re * sin)
        cols.append(jnp.concatenate([out_re, out_im], axis=0))
    y_hi, y_lo = split(jnp.concatenate(cols, axis=1))
    l_hi, l_lo = last[0], last[1]
    time = mm(jnp.concatenate([l_hi, l_hi], axis=1), jnp.concatenate([y_hi, y_lo], axis=0)) + mm(l_lo, y_hi)
    return [time[:, N * i : N * (i + 1)].T for i in range(count)]


def remote(src, dst, send, recv, device):
    return pltpu.make_async_remote_copy(
        src_ref=src, dst_ref=dst, send_sem=send, recv_sem=recv, device_id=device, device_id_type=MESH
    )


def build_band(taps_ref, band):
    rho = lax.broadcasted_iota(jnp.int32, (8, N), 0)
    lane = lax.broadcasted_iota(jnp.int32, (8, N), 1)
    shifted = 4 * lane - rho
    base = jnp.zeros((8, N), jnp.float32)
    for j in range(TAPS):
        base = jnp.where(shifted == j - 3, taps_ref[j], base)
    for t in range(BAND // 8):
        move = (2 * t - 32) % N
        tap = 4 * lane + (131 - 8 * t) - rho
        rolled = base if move == 0 else pltpu.roll(base, move, 1)
        band[8 * t : 8 * t + 8, :] = jnp.where((tap >= 0) & (tap < TAPS), rolled, 0.0)


def build_picker(index_ref):
    row = lax.broadcasted_iota(jnp.int32, (NSRC, 2 * GROUP), 0)
    wanted = jnp.zeros((NSRC, 2 * GROUP), jnp.int32)
    for s in range(NSRC):
        wanted = jnp.where(row == s, index_ref[s], wanted)
    owned = lax.broadcasted_iota(jnp.int32, (NSRC, 2 * GROUP), 1) % GROUP + lax.axis_index("chan") * GROUP
    return jnp.where(wanted == owned, 1.0, 0.0).astype(jnp.bfloat16)


def kernel(
    strain_hbm, taps_ref, index_ref, first_hbm, second_hbm, third_hbm, last_hbm, turn_hbm, win_hbm, back_hbm, out_ref,
    raw, band, dec, pick, pick_in, total, rs_in, acc, row_buf, rows_in, chan_in, src_all, spec_c, chan_op, spec, prod,
    first, second, third, last, turn, win, back,
    load_sem, own_sem, pick_sem, dec_send, dec_recv, rs_send, rs_recv, row_send, row_recv,
    g_send, g_recv, f_send, f_recv,
):
    tm = lax.axis_index("tm")
    ch = lax.axis_index("chan")
    x, zh = tm % 4, tm // 4
    y, zl, core = ch // 4, (ch // 2) % 2, ch % 2
    z, pair = 2 * zh + zl, ch // 2

    tables = (
        (first_hbm, first), (second_hbm, second), (third_hbm, third), (last_hbm, last), (turn_hbm, turn),
        (win_hbm, win), (back_hbm, back),
    )
    load = pltpu.make_async_copy(strain_hbm, raw.at[:, pl.ds(N, 4 * N * BLOCKS)], load_sem.at[0])
    load.start()
    loads = [pltpu.make_async_copy(a, b, load_sem.at[1 + i]) for i, (a, b) in enumerate(tables)]
    for copy in loads:
        copy.start()

    def device(axis, d):
        if axis == "x":
            return (zh * 4 + (x + d) % 4, ch)
        if axis == "y":
            return (tm, ((y + d) % 4) * 4 + zl * 2 + core)
        other = (z + d) % 4
        return ((other // 2) * 4 + x, y * 4 + (other % 2) * 2 + core)

    sibling = (tm, 2 * pair + 1 - core)
    peers = [sibling]
    peers += [(tm, 2 * ((pair + d) % 8) + core) for d in range(1, 8)]
    peers += [((tm + d) % TM, 2 * pair + (core + e) % 2) for d in range(1, TM) for e in range(2)]
    peers += [((1 - zh) * 4 + x, y * 4 + (1 - zl) * 2 + core)]
    barrier = pltpu.get_barrier_semaphore()
    for peer in peers:
        pl.semaphore_signal(barrier, inc=1, device_id=peer, device_id_type=MESH)

    raw[:, :N] = jnp.zeros((GROUP, N), jnp.float32)
    build_band(taps_ref, band)
    picker = build_picker(index_ref)
    b_hi, b_lo = split(band[...])
    both = jnp.concatenate([b_hi, b_lo], axis=1)
    load.wait()

    def finish(half, block, value):
        for j in range(TM):
            dec[j, half * HB + block] = value[8 * j : 8 * j + 8]
        picked = mm(picker, jnp.concatenate(split(value), axis=0))
        for j in range(NSRC // 8):
            pick[half, j, block] = picked[8 * j : 8 * j + 8]

    hi, lo = split(raw[:, 4 * N * BLOCKS :])
    wide = mm(hi, both[:N])
    finish(1, HB, wide[:, :N] + wide[:, N:] + mm(lo, b_hi[:N]))
    for j in range(NSRC // 8):
        pick[0, j, HB] = jnp.zeros((8, N), jnp.float32)

    def filter_half(half):
        for b0 in range(0, HB, 4):
            his, los = [], []
            for b in range(b0, b0 + 4):
                start = pl.multiple_of((half * HB + b) * (4 * N), 4 * N)
                hi, lo = split(raw[:, pl.ds(start, BAND)])
                his.append(hi)
                los.append(lo)
            hi, lo = jnp.concatenate(his, axis=0), jnp.concatenate(los, axis=0)
            wide = mm(hi, both)
            value = wide[:, :N] + wide[:, N:] + mm(lo, b_hi)
            for b in range(b0, b0 + 4):
                finish(half, b, value[GROUP * (b - b0) : GROUP * (b - b0 + 1)])

    started = []

    filter_half(1 - core)
    pl.semaphore_wait(barrier, len(peers))
    give = remote(pick.at[1 - core], pick_in, pick_sem.at[0], pick_sem.at[1], sibling)
    give.start()
    filter_half(core)
    own_blocks = pltpu.make_async_copy(dec.at[tm], chan_in.at[tm], own_sem.at[0])
    own_blocks.start()

    give.wait_recv()
    total[...] = pick[core] + pick_in[...]
    sums = []
    for d in (1, 7, 2, 6, 3, 5, 4):
        other = (pair + d) % 8
        copy = remote(total.at[other], rs_in.at[d], rs_send.at[d], rs_recv.at[d], (tm, 2 * other + core))
        copy.start()
        sums.append(copy)
    for copy in sums:
        copy.wait_recv()
    value = total[pair]
    for d in range(1, 8):
        value = value + rs_in[d]
    acc[...] = value.reshape(PART * 8, N)
    for j in range(TM):
        row_buf[j, :PART] = acc[pl.ds(j, PART, stride=8), :]
        row_buf[j, PART:] = jnp.zeros((16 - PART, N), jnp.float32)
    rows = []
    for d in range(TM):
        for e in range(2):
            if d == 0 and e == 0:
                continue
            other = (tm + d) % TM
            copy = remote(
                row_buf.at[other],
                rows_in.at[core, tm],
                row_send.at[d, e],
                row_recv.at[d, e],
                (other, 2 * pair + (core + e) % 2),
            )
            copy.start()
            rows.append(copy)
    rows_in[core, tm] = row_buf[tm]
    blocks = []
    for d in (1, 3, 2, 4, 5, 7, 6):
        other = (tm + d) % TM
        copy = remote(dec.at[other], chan_in.at[tm], dec_send.at[d], dec_recv.at[d], (other, ch))
        copy.start()
        blocks.append(copy)
    for copy in loads:
        copy.wait()
    for copy in rows:
        copy.wait_recv()
    place = lax.broadcasted_iota(jnp.int32, (HB, N), 0)
    pieces = []
    for j in range(TM):
        early = rows_in[0, j, :HB]
        if j > 0:
            early = early + jnp.where(place == 0, rows_in[1, j - 1, HB : HB + 1], 0.0)
        pieces += [early, rows_in[1, j, :HB]]
    src_all[0, 0, 0] = whiten_series([jnp.concatenate(pieces, axis=0)], first, second, third, last, turn)[0]

    REST = pl.ds(1, 3)

    def region(kind, offsets):
        start, size, order = KINDS[kind]
        at = dict(zip(order, offsets))
        return src_all.at[at["y"], at["z"], at["x"], pl.ds(core * HALF + start, size)]

    counts = [{}, {}]

    def number(which, key):
        return counts[which].setdefault(key, len(counts[which]))

    def placed(offsets, axis, d):
        return tuple((4 - d) if i == axis else o for i, o in enumerate(offsets))

    def tag(offsets):
        return tuple("*" if not isinstance(o, int) else o for o in offsets)

    def send_on(kind, offsets, axis):
        for d in ORDER:
            to = placed(offsets, axis, d)
            n = number(0, (kind, tag(to), axis))
            copy = remote(
                region(kind, offsets), region(kind, to), g_send.at[n], g_recv.at[n], device(KINDS[kind][2][axis], d)
            )
            copy.start()
            started.append(copy)

    def arrived(kind, offsets, axis, ds=ORDER):
        for d in ds:
            to = placed(offsets, axis, d)
            n = number(0, (kind, tag(to), axis))
            part = region(kind, to)
            remote(part, part, g_send.at[n], g_recv.at[n], sibling).wait_recv()

    def share(kind, offsets):
        part = region(kind, offsets)
        n = number(1, (kind, tag(offsets)))
        copy = remote(part, part, f_send.at[n], f_recv.at[n], sibling)
        copy.start()
        started.append(copy)
        shared.append(copy)

    def settle():
        for copy in shared:
            copy.wait_recv()
        shared.clear()

    shared = []
    kinds = range(3)
    for axis in range(3):
        for kind in kinds:
            send_on(kind, (0, 0, 0), axis)

    place = lax.broadcasted_iota(jnp.int32, (BLOCKS, N), 0)

    def channel(c):
        pieces = []
        for j in range(TM):
            value = chan_in[j, :BLOCKS, c, :]
            if j > 0:
                value = value + jnp.where(place == 0, chan_in[j - 1, BLOCKS, c : c + 1, :], 0.0)
            pieces.append(value)
        return jnp.concatenate(pieces, axis=0)

    def channels(c0):
        whites = whiten_series([channel(c) for c in range(c0, c0 + 4)], first, second, third, last, turn)
        data = [jnp.concatenate([w, pltpu.roll(w, N - 1, 1)], axis=0) for w in whites]
        res = mm3((win[0], win[1]), split(jnp.concatenate(data, axis=1)))
        for i in range(2 * N // 8):
            for c in range(4):
                at = 8 * (c0 + c)
                spec_c[i, at : at + 8] = res[8 * i : 8 * i + 8, N * c : N * (c + 1)]

    def channel_slots(i, carry):
        for k in range(8):
            re = spec_c[i, pl.ds(k, 8, stride=8), :]
            im = spec_c[i + N // 8, pl.ds(k, 8, stride=8), :]
            straight, crossed = (re, im), (im, -re)
            if k == 0:
                single = jnp.broadcast_to(i == 0, re.shape)
                straight = (re, jnp.where(single, 0.0, im))
                crossed = (jnp.where(single, 0.0, im), jnp.where(single, im, -re))
            whole = []
            for halves in (straight, crossed):
                for r in range(-LAG_ROWS // 2, LAG_ROWS // 2):
                    moved = [h if r == 0 else pltpu.roll(h, -r % N, 1) for h in halves]
                    whole.append(jnp.concatenate(moved, axis=1))
            hi, lo = split(jnp.concatenate(whole, axis=0))
            chan_op[i * 8 + k] = jnp.concatenate([hi, lo], axis=0)
        return carry

    for kind in kinds:
        arrived(kind, (0, 0, 0), 0)
        send_on(kind, (REST, 0, 0), 1)
        share(kind, (REST, 0, 0))
    for kind in kinds:
        arrived(kind, (0, 0, 0), 1)
        send_on(kind, (REST, 0, 0), 2)
        send_on(kind, (0, REST, 0), 2)
        share(kind, (0, REST, 0))
    for kind in kinds:
        arrived(kind, (0, 0, 0), 2)
        share(kind, (0, 0, REST))
    own_blocks.wait()
    for copy in blocks:
        copy.wait_recv()
    channels(0)
    for kind in kinds:
        arrived(kind, (REST, 0, 0), 1)
        send_on(kind, (REST, REST, 0), 2)
        share(kind, (REST, REST, 0))
    channels(4)
    lax.fori_loop(0, N // 8, channel_slots, 0)
    for kind in kinds:
        arrived(kind, (REST, 0, 0), 2)
        share(kind, (REST, 0, REST))
        arrived(kind, (0, REST, 0), 2)
        share(kind, (0, REST, REST))
    settle()

    w_hi, w_lo = win[0][:, :N], win[1][:, :N]
    w_both = jnp.concatenate([w_hi, w_hi], axis=1)

    def transform(places):
        hi, lo = split(jnp.concatenate([src_all[ry, rz, rx] for ry, rz, rx in places], axis=1))
        rows = []
        for ry, rz, rx in places:
            z_s = (z + rz) % 4
            source = 8 * (2 * ((y + ry) % 4) + z_s % 2) + 4 * (z_s // 2) + (x + rx) % 4
            rows.append(pl.ds(pl.multiple_of(source * 8, 8), 8))
        res = mm(w_both, jnp.concatenate([hi, lo], axis=0)) + mm(w_lo, hi)
        for i in range(2 * N // 8):
            for e, at in enumerate(rows):
                spec[i, at, :] = res[8 * i : 8 * i + 8, N * e : N * (e + 1)]

    def column(ry, carry):
        transform([(ry, rz, 0) for rz in range(4)])
        return carry

    def early(t, carry):
        ry = jnp.where(t < 4, t, 0)
        rz = jnp.where(t < 4, 0, t - 3)
        transform([(ry, rz, rx) for rx in range(1, 4)])
        return carry

    def late(ry, carry):
        transform([(ry, rz, rx) for rz in range(1, 4) for rx in range(1, 4)])
        return carry

    lax.fori_loop(0, 4, column, 0)
    lax.fori_loop(0, 7, early, 0)

    left = lax.broadcasted_iota(jnp.int32, (NSRC, N), 1) < HALF

    def slots(i, carry):
        for k in range(UNROLL):
            n = i * UNROLL + k
            tile = i * (UNROLL // 8) + k // 8
            re = spec[tile, pl.ds(k % 8, NSRC, stride=8), :]
            im = spec[tile + N // 8, pl.ds(k % 8, NSRC, stride=8), :]
            hi, lo = split(jnp.concatenate([re, im], axis=1))
            res = lax.dot_general(
                chan_op[n],
                jnp.concatenate([hi, lo], axis=0),
                (((1,), (1,)), ((), ())),
                preferred_element_type=jnp.float32,
            )
            u = res[:64] + jnp.where(left, res[64:], 0.0)
            v = u + pltpu.roll(u, HALF, 1)
            prod[pl.ds(pl.multiple_of(n * 32, 32), 32), :] = jnp.where(left[:32], v[:32], v[32:])
        return carry

    for kind in kinds:
        for d in ORDER:
            arrived(kind, (REST, REST, 0), 2, (d,))
            share(kind, (REST, REST, 4 - d))
    settle()
    lax.fori_loop(1, 4, late, 0)
    lax.fori_loop(0, N // UNROLL, slots, 0)

    k_hi = back[0]
    k_both = jnp.concatenate([back[0], back[1]], axis=1)
    for r in range(LAG_ROWS):
        for c in range(8):
            t = prod[pl.ds(r * 8 + c, N, stride=32), :].T
            hi, lo = split(jnp.concatenate([t[:NSRC], t[NSRC:]], axis=1))
            wide = mm(hi, k_both)
            out_ref[c, :, N * r : N * (r + 1)] = wide[:, :N] + wide[:, N:] + mm(lo, k_hi)

    give.wait_send()
    for copy in sums + rows + blocks + started:
        copy.wait_send()


def on_device(strain, fir_taps, source_index):
    tables = series_tables()
    win, back = window_tables()
    tables = [stack_np(t) for t in tables[:4]] + [tables[4], stack_np(win), stack_np(back)]
    dma = pltpu.SemaphoreType.DMA
    f32 = jnp.float32
    smem = pl.BlockSpec(memory_space=pltpu.SMEM)
    anywhere = pl.BlockSpec(memory_space=pl.ANY)
    return pl.pallas_call(
        kernel,
        out_shape=jax.ShapeDtypeStruct((8, NSRC, LAG_ROWS * N), f32),
        in_specs=[anywhere, smem, smem] + [anywhere] * len(tables),
        out_specs=pl.BlockSpec(memory_space=VMEM),
        scratch_shapes=[
            VMEM((GROUP, N + 4 * N * BLOCKS), f32),
            VMEM((BAND, N), f32),
            VMEM((TM, BLOCKS + 1, 8, N), f32),
            VMEM((2, 8, PART, 8, N), f32),
            VMEM((8, PART, 8, N), f32),
            VMEM((8, PART, 8, N), f32),
            VMEM((8, PART, 8, N), f32),
            VMEM((PART * 8, N), f32),
            VMEM((TM, 16, N), f32),
            VMEM((2, TM, 16, N), f32),
            VMEM((TM, BLOCKS + 1, 8, N), f32),
            VMEM((4, 4, 4, N, N), f32),
            VMEM((2 * N // 8, 64, N), f32),
            VMEM((N, N, 2 * N), jnp.bfloat16),
            VMEM((2 * N // 8, 8 * NSRC, N), f32),
            VMEM((N * 32, N), f32),
        ]
        + [VMEM(t.shape, jnp.dtype(t.dtype)) for t in tables]
        + [
            dma((1 + len(tables),)),
            dma((1,)),
            dma((2,)),
            dma((TM,)),
            dma((TM,)),
            dma((8,)),
            dma((8,)),
            dma((TM, 2)),
            dma((TM, 2)),
        ]
        + [dma((81,))] * 2
        + [dma((27,))] * 2,
        compiler_params=pltpu.CompilerParams(
            collective_id=0, has_side_effects=True, vmem_limit_bytes=VMEM_LIMIT
        ),
        name="interferometry",
    )(strain, fir_taps, source_index, *tables)


def solution(mesh):
    return jax.shard_map(
        on_device,
        mesh=mesh,
        in_specs=(P("chan", "tm"), P(), P()),
        out_specs=P(("chan", "tm"), None, None),
        check_vma=False,
    )
```

```python
import functools

import jax
import jax.numpy as jnp
import ml_dtypes
import numpy as np
from jax import lax
from jax.experimental import pallas as pl
from jax.experimental.pallas import tpu as pltpu
from jax.sharding import PartitionSpec as P

MESH = pl.DeviceIdType.MESH
VMEM = pltpu.VMEM
N = 128
NT = N * N
HALF = N // 2
TAPS = 64
NSRC = 64
FLOOR = 0.1
LAG_ROWS = 4
GROUP = 64
TM = 8
BLOCKS = 16
BAND = 5 * N
HB = BLOCKS // 2
PART = HB + 1
KINDS = ((0, 24, "xyz"), (24, 24, "yzx"), (48, 16, "zxy"))
ORDER = (1, 3, 2)
UNROLL = 64
VMEM_LIMIT = 56 * 1024 * 1024


def split_np(table):
    high = table.astype(np.float32).astype(ml_dtypes.bfloat16)
    low = (table - high.astype(np.float64)).astype(np.float32).astype(ml_dtypes.bfloat16)
    return high, low


def stack_np(table):
    return np.stack(split_np(table))


def series_tables():
    k = np.arange(HALF)[:, None]
    q = np.arange(N)[None, :]
    ang = 2 * np.pi * ((k * q) % N) / N
    first = np.concatenate([np.cos(ang), -np.sin(ang)])
    first[HALF] = np.cos(np.pi * np.arange(N))
    ang = 2 * np.pi * ((np.arange(N)[:, None] * np.arange(N)[None, :]) % N) / N
    c, s = np.cos(ang), np.sin(ang)
    second = np.block([[c, -s], [s, c]])
    third = np.block([[c, s], [-s, c]])
    ang = 2 * np.pi * ((np.arange(N)[:, None] * np.arange(HALF)[None, :]) % N) / N
    last = np.concatenate([2 * np.cos(ang), -2 * np.sin(ang)], axis=1) / N
    last[:, 0] = 1.0 / N
    last[:, HALF] = np.cos(np.pi * np.arange(N)) / N
    ang = 2 * np.pi * (np.arange(HALF + 8)[:, None] * np.arange(N)[None, :]) / NT
    turn = np.stack([np.cos(ang), np.sin(ang)]).astype(np.float32)
    return first, second, third, last, turn


def window_tables():
    f = np.arange(N)[:, None]
    u = np.arange(2 * N)[None, :]
    ang = 2 * np.pi * ((f * u) % (2 * N)) / (2 * N)
    win = np.concatenate([np.cos(ang), -np.sin(ang)])
    win[N] = np.cos(np.pi * np.arange(2 * N))
    m = np.arange(N)[None, :]
    ang = 2 * np.pi * ((f * m) % (2 * N)) / (2 * N)
    scale = 1.0 / (2 * N * N)
    back = np.concatenate([2 * np.cos(ang), -2 * np.sin(ang)]) * scale
    back[0] = scale
    back[N] = np.cos(np.pi * np.arange(N)) * scale
    return win, back


def split(value):
    high = value.astype(jnp.bfloat16)
    low = (value - high.astype(jnp.float32)).astype(jnp.bfloat16)
    return high, low


def mm(a, b):
    return jnp.dot(a, b, preferred_element_type=jnp.float32)


def mm3(a, b):
    return mm(a[0], b[0]) + mm(a[0], b[1]) + mm(a[1], b[0])


def whiten_series(series, first, second, third, last, turn):
    count = len(series)
    powers = [jnp.sum(x * x) for x in series]
    x_hi, x_lo = split(jnp.concatenate(series, axis=1))
    a_hi, a_lo = first[0], first[1]
    part = mm(jnp.concatenate([a_hi, a_hi], axis=1), jnp.concatenate([x_hi, x_lo], axis=0)) + mm(a_lo, x_hi)
    cos, sin = turn[0, :HALF], turn[1, :HALF]
    cos_mid, sin_mid = turn[0, HALF : HALF + 1], turn[1, HALF : HALF + 1]
    top = lax.broadcasted_iota(jnp.int32, (HALF, N), 0) == 0
    cos_im = jnp.where(top, 0.0, cos)
    rows, mids = [], []
    for i in range(count):
        re = part[:HALF, N * i : N * (i + 1)]
        im = part[HALF:, N * i : N * (i + 1)]
        rows.append(jnp.concatenate([re * cos + im * sin, im * cos_im - re * sin], axis=1))
        mid = im[:1]
        mids.append(jnp.concatenate([mid * cos_mid, -mid * sin_mid], axis=1))
    pad = -count % 8
    if pad:
        mids.append(jnp.zeros((pad, 2 * N), jnp.float32))
    turned = jnp.concatenate(rows + mids, axis=0)
    spec = mm3(split(turned), (second[0], second[1]))
    spec_re, spec_im = spec[:, :N], spec[:, N:]
    energy = spec_re * spec_re + spec_im * spec_im
    floor = [jnp.broadcast_to(FLOOR * p, (HALF, N)) for p in powers]
    floor += [jnp.broadcast_to(FLOOR * p, (1, N)) for p in powers]
    if pad:
        floor.append(jnp.ones((pad, N), jnp.float32))
    scale = lax.rsqrt(energy + jnp.concatenate(floor, axis=0))
    white = jnp.concatenate([spec_re * scale, spec_im * scale], axis=1)
    back = mm3(split(white), (third[0], third[1]))
    cols = []
    for i in range(count):
        re = back[HALF * i : HALF * (i + 1), :N]
        im = back[HALF * i : HALF * (i + 1), N:]
        mid = HALF * count + i
        mid_re, mid_im = back[mid : mid + 1, :N], back[mid : mid + 1, N:]
        out_re = re * cos - im * sin
        out_im = jnp.where(top, mid_re * cos_mid - mid_im * sin_mid, im * cos + re * sin)
        cols.append(jnp.concatenate([out_re, out_im], axis=0))
    y_hi, y_lo = split(jnp.concatenate(cols, axis=1))
    l_hi, l_lo = last[0], last[1]
    time = mm(jnp.concatenate([l_hi, l_hi], axis=1), jnp.concatenate([y_hi, y_lo], axis=0)) + mm(l_lo, y_hi)
    return [time[:, N * i : N * (i + 1)].T for i in range(count)]


def remote(src, dst, send, recv, device):
    return pltpu.make_async_remote_copy(
        src_ref=src, dst_ref=dst, send_sem=send, recv_sem=recv, device_id=device, device_id_type=MESH
    )


def build_band(taps_ref, band):
    rho = lax.broadcasted_iota(jnp.int32, (8, N), 0)
    lane = lax.broadcasted_iota(jnp.int32, (8, N), 1)
    shifted = 4 * lane - rho
    base = jnp.zeros((8, N), jnp.float32)
    for j in range(TAPS):
        base = jnp.where(shifted == j - 3, taps_ref[j], base)
    for t in range(BAND // 8):
        move = (2 * t - 32) % N
        tap = 4 * lane + (131 - 8 * t) - rho
        rolled = base if move == 0 else pltpu.roll(base, move, 1)
        band[8 * t : 8 * t + 8, :] = jnp.where((tap >= 0) & (tap < TAPS), rolled, 0.0)


def build_picker(index_ref):
    row = lax.broadcasted_iota(jnp.int32, (NSRC, 2 * GROUP), 0)
    wanted = jnp.zeros((NSRC, 2 * GROUP), jnp.int32)
    for s in range(NSRC):
        wanted = jnp.where(row == s, index_ref[s], wanted)
    owned = lax.broadcasted_iota(jnp.int32, (NSRC, 2 * GROUP), 1) % GROUP + lax.axis_index("chan") * GROUP
    return jnp.where(wanted == owned, 1.0, 0.0).astype(jnp.bfloat16)


def kernel(
    strain_hbm, taps_ref, index_ref, first_hbm, second_hbm, third_hbm, last_hbm, turn_hbm, win_hbm, out_hbm,
    raw, band, dec, pick, pick_in, total, rs_in, acc, row_buf, rows_in, halves, chan_in, src_all, spec_c, chan_op, spec, prod,
    first, second, third, last, turn, win,
    load_sem, own_sem, pick_sem, dec_send, dec_recv, rs_send, rs_recv, row_send, row_recv,
    g_send, g_recv, f_send, f_recv, out_sem,
):
    tm = lax.axis_index("tm")
    ch = lax.axis_index("chan")
    x, zh = tm % 4, tm // 4
    y, zl, core = ch // 4, (ch // 2) % 2, ch % 2
    z, pair = 2 * zh + zl, ch // 2

    tables = (
        (first_hbm, first), (second_hbm, second), (third_hbm, third), (last_hbm, last), (turn_hbm, turn),
        (win_hbm, win),
    )
    load = pltpu.make_async_copy(strain_hbm, raw.at[:, pl.ds(N, 4 * N * BLOCKS)], load_sem.at[0])
    load.start()
    loads = [pltpu.make_async_copy(a, b, load_sem.at[1 + i]) for i, (a, b) in enumerate(tables)]
    for copy in loads:
        copy.start()

    def device(axis, d):
        if axis == "x":
            return (zh * 4 + (x + d) % 4, ch)
        if axis == "y":
            return (tm, ((y + d) % 4) * 4 + zl * 2 + core)
        other = (z + d) % 4
        return ((other // 2) * 4 + x, y * 4 + (other % 2) * 2 + core)

    sibling = (tm, 2 * pair + 1 - core)
    plane = 8 * zl + tm

    def in_plane(n):
        return (n % TM, 4 * y + 2 * (n // TM) + core)

    peers = [sibling]
    peers += [device("y", d) for d in ORDER]
    peers += [in_plane((plane + d) % 16) for d in range(1, 16)]
    barrier = pltpu.get_barrier_semaphore()
    for peer in peers:
        pl.semaphore_signal(barrier, inc=1, device_id=peer, device_id_type=MESH)

    raw[:, :N] = jnp.zeros((GROUP, N), jnp.float32)
    build_band(taps_ref, band)
    picker = build_picker(index_ref)
    b_hi, b_lo = split(band[...])
    both = jnp.concatenate([b_hi, b_lo], axis=1)
    load.wait()

    def finish(half, block, value):
        for j in range(TM):
            dec[j, half * HB + block] = value[8 * j : 8 * j + 8]
        picked = mm(picker, jnp.concatenate(split(value), axis=0))
        for j in range(NSRC // 8):
            pick[half, j, block] = picked[8 * j : 8 * j + 8]

    hi, lo = split(raw[:, 4 * N * BLOCKS :])
    wide = mm(hi, both[:N])
    finish(1, HB, wide[:, :N] + wide[:, N:] + mm(lo, b_hi[:N]))
    for j in range(NSRC // 8):
        pick[0, j, HB] = jnp.zeros((8, N), jnp.float32)

    def filter_half(half):
        for b0 in range(0, HB, 4):
            his, los = [], []
            for b in range(b0, b0 + 4):
                start = pl.multiple_of((half * HB + b) * (4 * N), 4 * N)
                hi, lo = split(raw[:, pl.ds(start, BAND)])
                his.append(hi)
                los.append(lo)
            hi, lo = jnp.concatenate(his, axis=0), jnp.concatenate(los, axis=0)
            wide = mm(hi, both)
            value = wide[:, :N] + wide[:, N:] + mm(lo, b_hi)
            for b in range(b0, b0 + 4):
                finish(half, b, value[GROUP * (b - b0) : GROUP * (b - b0 + 1)])

    started = []

    filter_half(1 - core)
    pl.semaphore_wait(barrier, len(peers))
    give = remote(pick.at[1 - core], pick_in, pick_sem.at[0], pick_sem.at[1], sibling)
    give.start()
    filter_half(core)
    own_blocks = pltpu.make_async_copy(dec.at[tm], chan_in.at[tm], own_sem.at[0])
    own_blocks.start()

    blocks = []
    for d in (1, 3, 2, 4, 5, 7, 6):
        other = (tm + d) % TM
        copy = remote(dec.at[other], chan_in.at[tm], dec_send.at[d], dec_recv.at[d], (other, ch))
        copy.start()
        blocks.append(copy)
    give.wait_recv()
    total[...] = pick[core] + pick_in[...]
    sums = []
    for d in ORDER:
        copy = remote(
            total.at[pl.ds(2 * ((y + d) % 4), 2)], rs_in.at[d], rs_send.at[d], rs_recv.at[d], device("y", d)
        )
        copy.start()
        sums.append(copy)
    for copy in sums:
        copy.wait_recv()
    acc[...] = (total[pl.ds(2 * y, 2)] + rs_in[1] + rs_in[2] + rs_in[3]).reshape(2 * PART * 8, N)
    for n in range(16):
        row_buf[n, :PART] = acc[pl.ds((n // TM) * PART * 8 + n % TM, PART, stride=8), :]
        row_buf[n, PART:] = jnp.zeros((16 - PART, N), jnp.float32)
    rows = []
    for d in range(1, 16):
        other = (plane + d) % 16
        copy = remote(row_buf.at[other], rows_in.at[zl, tm], row_send.at[d], row_recv.at[d], in_plane(other))
        copy.start()
        rows.append(copy)
    rows_in[zl, tm] = row_buf[plane]
    for copy in loads:
        copy.wait()
    for copy in rows:
        copy.wait_recv()
    halves[core] = rows_in[0] + rows_in[1]
    swap = remote(halves.at[core], halves.at[core], pick_sem.at[2], pick_sem.at[3], sibling)
    swap.start()
    swap.wait_recv()
    place = lax.broadcasted_iota(jnp.int32, (HB, N), 0)
    pieces = []
    for j in range(TM):
        early = halves[0, j, :HB]
        if j > 0:
            early = early + jnp.where(place == 0, halves[1, j - 1, HB : HB + 1], 0.0)
        pieces += [early, halves[1, j, :HB]]
    src_all[0, 0, 0] = whiten_series([jnp.concatenate(pieces, axis=0)], first, second, third, last, turn)[0]

    REST = pl.ds(1, 3)

    def region(kind, offsets):
        start, size, order = KINDS[kind]
        at = dict(zip(order, offsets))
        return src_all.at[at["y"], at["z"], at["x"], pl.ds(core * HALF + start, size)]

    counts = [{}, {}]

    def number(which, key):
        return counts[which].setdefault(key, len(counts[which]))

    def placed(offsets, axis, d):
        return tuple((4 - d) if i == axis else o for i, o in enumerate(offsets))

    def tag(offsets):
        return tuple("*" if not isinstance(o, int) else o for o in offsets)

    def send_on(kind, offsets, axis):
        for d in ORDER:
            to = placed(offsets, axis, d)
            n = number(0, (kind, tag(to), axis))
            copy = remote(
                region(kind, offsets), region(kind, to), g_send.at[n], g_recv.at[n], device(KINDS[kind][2][axis], d)
            )
            copy.start()
            started.append(copy)

    def arrived(kind, offsets, axis, ds=ORDER):
        for d in ds:
            to = placed(offsets, axis, d)
            n = number(0, (kind, tag(to), axis))
            part = region(kind, to)
            remote(part, part, g_send.at[n], g_recv.at[n], sibling).wait_recv()

    def share(kind, offsets):
        part = region(kind, offsets)
        n = number(1, (kind, tag(offsets)))
        copy = remote(part, part, f_send.at[n], f_recv.at[n], sibling)
        copy.start()
        started.append(copy)
        shared.append(copy)

    def settle():
        for copy in shared:
            copy.wait_recv()
        shared.clear()

    shared = []
    kinds = range(3)
    for axis in range(3):
        for kind in kinds:
            send_on(kind, (0, 0, 0), axis)

    place = lax.broadcasted_iota(jnp.int32, (BLOCKS, N), 0)

    def channel(c):
        pieces = []
        for j in range(TM):
            value = chan_in[j, :BLOCKS, c, :]
            if j > 0:
                value = value + jnp.where(place == 0, chan_in[j - 1, BLOCKS, c : c + 1, :], 0.0)
            pieces.append(value)
        return jnp.concatenate(pieces, axis=0)

    def channels(c0):
        whites = whiten_series([channel(c) for c in range(c0, c0 + 4)], first, second, third, last, turn)
        data = [jnp.concatenate([w, pltpu.roll(w, N - 1, 1)], axis=0) for w in whites]
        res = mm3((win[0], win[1]), split(jnp.concatenate(data, axis=1)))
        for i in range(2 * N // 8):
            for c in range(4):
                at = 8 * (c0 + c)
                spec_c[i, at : at + 8] = res[8 * i : 8 * i + 8, N * c : N * (c + 1)]

    def channel_slots(i, carry):
        for k in range(8):
            re = spec_c[i, pl.ds(k, 8, stride=8), :]
            im = spec_c[i + N // 8, pl.ds(k, 8, stride=8), :]
            straight, crossed = (re, im), (im, -re)
            if k == 0:
                single = jnp.broadcast_to(i == 0, re.shape)
                straight = (re, jnp.where(single, 0.0, im))
                crossed = (jnp.where(single, 0.0, im), jnp.where(single, im, -re))
            whole = []
            for halves in (straight, crossed):
                for r in range(-LAG_ROWS // 2, LAG_ROWS // 2):
                    moved = [h if r == 0 else pltpu.roll(h, -r % N, 1) for h in halves]
                    whole.append(jnp.concatenate(moved, axis=1))
            hi, lo = split(jnp.concatenate(whole, axis=0))
            chan_op[i * 8 + k] = jnp.concatenate([hi, lo], axis=0)
        return carry

    for kind in kinds:
        arrived(kind, (0, 0, 0), 0)
        send_on(kind, (REST, 0, 0), 1)
        share(kind, (REST, 0, 0))
    for kind in kinds:
        arrived(kind, (0, 0, 0), 1)
        send_on(kind, (REST, 0, 0), 2)
        send_on(kind, (0, REST, 0), 2)
        share(kind, (0, REST, 0))
    for kind in kinds:
        arrived(kind, (0, 0, 0), 2)
        share(kind, (0, 0, REST))
    own_blocks.wait()
    for copy in blocks:
        copy.wait_recv()
    channels(0)
    for kind in kinds:
        arrived(kind, (REST, 0, 0), 1)
        send_on(kind, (REST, REST, 0), 2)
        share(kind, (REST, REST, 0))
    channels(4)
    lax.fori_loop(0, N // 8, channel_slots, 0)
    for kind in kinds:
        arrived(kind, (REST, 0, 0), 2)
        share(kind, (REST, 0, REST))
        arrived(kind, (0, REST, 0), 2)
        share(kind, (0, REST, REST))
    settle()

    w_hi, w_lo = win[0][:, :N], win[1][:, :N]
    w_both = jnp.concatenate([w_hi, w_hi], axis=1)

    def transform(places):
        hi, lo = split(jnp.concatenate([src_all[ry, rz, rx] for ry, rz, rx in places], axis=1))
        rows = []
        for ry, rz, rx in places:
            z_s = (z + rz) % 4
            source = 8 * (2 * ((y + ry) % 4) + z_s % 2) + 4 * (z_s // 2) + (x + rx) % 4
            rows.append(pl.ds(pl.multiple_of(source * 8, 8), 8))
        res = mm(w_both, jnp.concatenate([hi, lo], axis=0)) + mm(w_lo, hi)
        for i in range(2 * N // 8):
            for e, at in enumerate(rows):
                spec[i, at, :] = res[8 * i : 8 * i + 8, N * e : N * (e + 1)]

    def column(ry, carry):
        transform([(ry, rz, 0) for rz in range(4)])
        return carry

    def early(t, carry):
        ry = jnp.where(t < 4, t, 0)
        rz = jnp.where(t < 4, 0, t - 3)
        transform([(ry, rz, rx) for rx in range(1, 4)])
        return carry

    def late(ry, carry):
        transform([(ry, rz, rx) for rz in range(1, 4) for rx in range(1, 4)])
        return carry

    lax.fori_loop(0, 4, column, 0)
    lax.fori_loop(0, 7, early, 0)

    left = lax.broadcasted_iota(jnp.int32, (NSRC, N), 1) < HALF

    def slots(i, carry):
        for k in range(UNROLL):
            n = i * UNROLL + k
            tile = i * (UNROLL // 8) + k // 8
            re = spec[tile, pl.ds(k % 8, NSRC, stride=8), :]
            im = spec[tile + N // 8, pl.ds(k % 8, NSRC, stride=8), :]
            hi, lo = split(jnp.concatenate([re, im], axis=1))
            res = lax.dot_general(
                chan_op[n],
                jnp.concatenate([hi, lo], axis=0),
                (((1,), (1,)), ((), ())),
                preferred_element_type=jnp.float32,
            )
            u = res[:64] + jnp.where(left, res[64:], 0.0)
            v = u + pltpu.roll(u, HALF, 1)
            prod[n] = jnp.where(left[:32], v[:32], v[32:]).reshape(LAG_ROWS, 8, N)
        part = pl.ds(i * UNROLL, UNROLL)
        pltpu.make_async_copy(prod.at[part], out_hbm.at[part], out_sem.at[i]).start()
        return carry

    for d in ORDER:
        for kind in kinds:
            arrived(kind, (REST, REST, 0), 2, (d,))
            share(kind, (REST, REST, 4 - d))
    settle()
    lax.fori_loop(1, 4, late, 0)
    lax.fori_loop(0, N // UNROLL, slots, 0)

    for i in range(N // UNROLL):
        part = pl.ds(i * UNROLL, UNROLL)
        pltpu.make_async_copy(prod.at[part], out_hbm.at[part], out_sem.at[i]).wait()
    swap.wait_send()
    give.wait_send()
    for copy in sums + rows + blocks + started:
        copy.wait_send()


def lags_kernel(prod_ref, back, out_ref):
    k_hi = back[0]
    k_both = jnp.concatenate([back[0], back[1]], axis=1)
    for c in range(8):
        t = prod_ref[:, 0, c, :].T
        hi, lo = split(jnp.concatenate([t[:NSRC], t[NSRC:]], axis=1))
        wide = mm(hi, k_both)
        out_ref[c] = wide[:, :N] + wide[:, N:] + mm(lo, k_hi)


def on_device(strain, fir_taps, source_index):
    tables = series_tables()
    win, back = window_tables()
    tables = [stack_np(t) for t in tables[:4]] + [tables[4], stack_np(win)]
    dma = pltpu.SemaphoreType.DMA
    f32 = jnp.float32
    smem = pl.BlockSpec(memory_space=pltpu.SMEM)
    anywhere = pl.BlockSpec(memory_space=pl.ANY)
    products = pl.pallas_call(
        kernel,
        out_shape=jax.ShapeDtypeStruct((N, LAG_ROWS, 8, N), f32),
        in_specs=[anywhere, smem, smem] + [anywhere] * len(tables),
        out_specs=anywhere,
        scratch_shapes=[
            VMEM((GROUP, N + 4 * N * BLOCKS), f32),
            VMEM((BAND, N), f32),
            VMEM((TM, BLOCKS + 1, 8, N), f32),
            VMEM((2, 8, PART, 8, N), f32),
            VMEM((8, PART, 8, N), f32),
            VMEM((8, PART, 8, N), f32),
            VMEM((4, 2, PART, 8, N), f32),
            VMEM((2 * PART * 8, N), f32),
            VMEM((16, 16, N), f32),
            VMEM((2, TM, 16, N), f32),
            VMEM((2, TM, 16, N), f32),
            VMEM((TM, BLOCKS + 1, 8, N), f32),
            VMEM((4, 4, 4, N, N), f32),
            VMEM((2 * N // 8, 64, N), f32),
            VMEM((N, N, 2 * N), jnp.bfloat16),
            VMEM((2 * N // 8, 8 * NSRC, N), f32),
            VMEM((N, LAG_ROWS, 8, N), f32),
        ]
        + [VMEM(t.shape, jnp.dtype(t.dtype)) for t in tables]
        + [
            dma((1 + len(tables),)),
            dma((2,)),
            dma((4,)),
            dma((TM,)),
            dma((TM,)),
            dma((4,)),
            dma((4,)),
            dma((16,)),
            dma((16,)),
        ]
        + [dma((81,))] * 2
        + [dma((27,))] * 2
        + [dma((N // UNROLL,))],
        compiler_params=pltpu.CompilerParams(
            collective_id=0, has_side_effects=True, vmem_limit_bytes=VMEM_LIMIT
        ),
        name="interferometry",
    )(strain, fir_taps, source_index, *tables)
    return pl.pallas_call(
        lags_kernel,
        grid=(LAG_ROWS,),
        out_shape=jax.ShapeDtypeStruct((8, NSRC, LAG_ROWS * N), f32),
        in_specs=[
            pl.BlockSpec((N, 1, 8, N), lambda r: (0, r, 0, 0)),
            pl.BlockSpec((2, 2 * N, N), lambda r: (0, 0, 0)),
        ],
        out_specs=pl.BlockSpec((8, NSRC, N), lambda r: (0, 0, r)),
        compiler_params=pltpu.CompilerParams(vmem_limit_bytes=VMEM_LIMIT),
        name="lags",
    )(products, stack_np(back))


def solution(mesh):
    return jax.shard_map(
        on_device,
        mesh=mesh,
        in_specs=(P("chan", "tm"), P(), P()),
        out_specs=P(("chan", "tm"), None, None),
        check_vma=False,
    )
```

```python
import functools

import jax
import jax.numpy as jnp
import ml_dtypes
import numpy as np
from jax import lax
from jax.experimental import pallas as pl
from jax.experimental.pallas import tpu as pltpu
from jax.sharding import PartitionSpec as P

MESH = pl.DeviceIdType.MESH
VMEM = pltpu.VMEM
N = 128
NT = N * N
HALF = N // 2
TAPS = 64
NSRC = 64
FLOOR = 0.1
LAG_ROWS = 4
GROUP = 64
TM = 8
BLOCKS = 16
BAND = 5 * N
HB = BLOCKS // 2
PART = HB + 1
KINDS = ((0, 24, "xyz"), (24, 16, "yzx"), (40, 24, "zxy"))
ORDER = (1, 3, 2)
UNROLL = 64
VMEM_LIMIT = 56 * 1024 * 1024


def split_np(table):
    high = table.astype(np.float32).astype(ml_dtypes.bfloat16)
    low = (table - high.astype(np.float64)).astype(np.float32).astype(ml_dtypes.bfloat16)
    return high, low


def stack_np(table):
    return np.stack(split_np(table))


def series_tables():
    k = np.arange(HALF)[:, None]
    q = np.arange(N)[None, :]
    ang = 2 * np.pi * ((k * q) % N) / N
    first = np.concatenate([np.cos(ang), -np.sin(ang)])
    first[HALF] = np.cos(np.pi * np.arange(N))
    ang = 2 * np.pi * ((np.arange(N)[:, None] * np.arange(N)[None, :]) % N) / N
    c, s = np.cos(ang), np.sin(ang)
    second = np.block([[c, -s], [s, c]])
    third = np.block([[c, s], [-s, c]])
    ang = 2 * np.pi * ((np.arange(N)[:, None] * np.arange(HALF)[None, :]) % N) / N
    last = np.concatenate([2 * np.cos(ang), -2 * np.sin(ang)], axis=1) / N
    last[:, 0] = 1.0 / N
    last[:, HALF] = np.cos(np.pi * np.arange(N)) / N
    ang = 2 * np.pi * (np.arange(HALF + 8)[:, None] * np.arange(N)[None, :]) / NT
    turn = np.stack([np.cos(ang), np.sin(ang)]).astype(np.float32)
    return first, second, third, last, turn


def window_tables():
    f = np.arange(N)[:, None]
    u = np.arange(2 * N)[None, :]
    ang = 2 * np.pi * ((f * u) % (2 * N)) / (2 * N)
    win = np.concatenate([np.cos(ang), -np.sin(ang)])
    win[N] = np.cos(np.pi * np.arange(2 * N))
    m = np.arange(N)[None, :]
    ang = 2 * np.pi * ((f * m) % (2 * N)) / (2 * N)
    scale = 1.0 / (2 * N * N)
    back = np.concatenate([2 * np.cos(ang), -2 * np.sin(ang)]) * scale
    back[0] = scale
    back[N] = np.cos(np.pi * np.arange(N)) * scale
    return win, back


def split(value):
    high = value.astype(jnp.bfloat16)
    low = (value - high.astype(jnp.float32)).astype(jnp.bfloat16)
    return high, low


def mm(a, b):
    return jnp.dot(a, b, preferred_element_type=jnp.float32)


def mm3(a, b):
    return mm(a[0], b[0]) + mm(a[0], b[1]) + mm(a[1], b[0])


def whiten_series(series, first, second, third, last, turn):
    count = len(series)
    powers = [jnp.sum(x * x) for x in series]
    x_hi, x_lo = split(jnp.concatenate(series, axis=1))
    a_hi, a_lo = first[0], first[1]
    part = mm(jnp.concatenate([a_hi, a_hi], axis=1), jnp.concatenate([x_hi, x_lo], axis=0)) + mm(a_lo, x_hi)
    cos, sin = turn[0, :HALF], turn[1, :HALF]
    cos_mid, sin_mid = turn[0, HALF : HALF + 1], turn[1, HALF : HALF + 1]
    top = lax.broadcasted_iota(jnp.int32, (HALF, N), 0) == 0
    cos_im = jnp.where(top, 0.0, cos)
    rows, mids = [], []
    for i in range(count):
        re = part[:HALF, N * i : N * (i + 1)]
        im = part[HALF:, N * i : N * (i + 1)]
        rows.append(jnp.concatenate([re * cos + im * sin, im * cos_im - re * sin], axis=1))
        mid = im[:1]
        mids.append(jnp.concatenate([mid * cos_mid, -mid * sin_mid], axis=1))
    pad = -count % 8
    if pad:
        mids.append(jnp.zeros((pad, 2 * N), jnp.float32))
    turned = jnp.concatenate(rows + mids, axis=0)
    spec = mm3(split(turned), (second[0], second[1]))
    spec_re, spec_im = spec[:, :N], spec[:, N:]
    energy = spec_re * spec_re + spec_im * spec_im
    floor = [jnp.broadcast_to(FLOOR * p, (HALF, N)) for p in powers]
    floor += [jnp.broadcast_to(FLOOR * p, (1, N)) for p in powers]
    if pad:
        floor.append(jnp.ones((pad, N), jnp.float32))
    scale = lax.rsqrt(energy + jnp.concatenate(floor, axis=0))
    white = jnp.concatenate([spec_re * scale, spec_im * scale], axis=1)
    back = mm3(split(white), (third[0], third[1]))
    cols = []
    for i in range(count):
        re = back[HALF * i : HALF * (i + 1), :N]
        im = back[HALF * i : HALF * (i + 1), N:]
        mid = HALF * count + i
        mid_re, mid_im = back[mid : mid + 1, :N], back[mid : mid + 1, N:]
        out_re = re * cos - im * sin
        out_im = jnp.where(top, mid_re * cos_mid - mid_im * sin_mid, im * cos + re * sin)
        cols.append(jnp.concatenate([out_re, out_im], axis=0))
    y_hi, y_lo = split(jnp.concatenate(cols, axis=1))
    l_hi, l_lo = last[0], last[1]
    time = mm(jnp.concatenate([l_hi, l_hi], axis=1), jnp.concatenate([y_hi, y_lo], axis=0)) + mm(l_lo, y_hi)
    return [time[:, N * i : N * (i + 1)].T for i in range(count)]


def remote(src, dst, send, recv, device):
    return pltpu.make_async_remote_copy(
        src_ref=src, dst_ref=dst, send_sem=send, recv_sem=recv, device_id=device, device_id_type=MESH
    )


def build_band(taps_ref, band):
    rho = lax.broadcasted_iota(jnp.int32, (8, N), 0)
    lane = lax.broadcasted_iota(jnp.int32, (8, N), 1)
    shifted = 4 * lane - rho
    base = jnp.zeros((8, N), jnp.float32)
    for j in range(TAPS):
        base = jnp.where(shifted == j - 3, taps_ref[j], base)
    for t in range(BAND // 8):
        move = (2 * t - 32) % N
        tap = 4 * lane + (131 - 8 * t) - rho
        rolled = base if move == 0 else pltpu.roll(base, move, 1)
        band[8 * t : 8 * t + 8, :] = jnp.where((tap >= 0) & (tap < TAPS), rolled, 0.0)


def build_picker(index_ref):
    row = lax.broadcasted_iota(jnp.int32, (NSRC, 2 * GROUP), 0)
    wanted = jnp.zeros((NSRC, 2 * GROUP), jnp.int32)
    for s in range(NSRC):
        wanted = jnp.where(row == s, index_ref[s], wanted)
    owned = lax.broadcasted_iota(jnp.int32, (NSRC, 2 * GROUP), 1) % GROUP + lax.axis_index("chan") * GROUP
    return jnp.where(wanted == owned, 1.0, 0.0).astype(jnp.bfloat16)


def kernel(
    strain_hbm, taps_ref, index_ref, first_hbm, second_hbm, third_hbm, last_hbm, turn_hbm, win_hbm, out_hbm,
    raw, band, dec, pick, pick_in, total, rs_in, acc, row_buf, rows_in, halves, chan_in, src_all, spec_c, chan_op, spec, prod,
    first, second, third, last, turn, win,
    load_sem, own_sem, pick_sem, dec_send, dec_recv, rs_send, rs_recv, row_send, row_recv,
    g_send, g_recv, f_send, f_recv, out_sem,
):
    tm = lax.axis_index("tm")
    ch = lax.axis_index("chan")
    x, zh = tm % 4, tm // 4
    y, zl, core = ch // 4, (ch // 2) % 2, ch % 2
    z, pair = 2 * zh + zl, ch // 2

    tables = (
        (first_hbm, first), (second_hbm, second), (third_hbm, third), (last_hbm, last), (turn_hbm, turn),
        (win_hbm, win),
    )
    load = pltpu.make_async_copy(strain_hbm, raw.at[:, pl.ds(N, 4 * N * BLOCKS)], load_sem.at[0])
    load.start()
    loads = [pltpu.make_async_copy(a, b, load_sem.at[1 + i]) for i, (a, b) in enumerate(tables)]
    for copy in loads:
        copy.start()

    def device(axis, d):
        if axis == "x":
            return (zh * 4 + (x + d) % 4, ch)
        if axis == "y":
            return (tm, ((y + d) % 4) * 4 + zl * 2 + core)
        other = (z + d) % 4
        return ((other // 2) * 4 + x, y * 4 + (other % 2) * 2 + core)

    sibling = (tm, 2 * pair + 1 - core)
    plane = 8 * zl + tm

    def in_plane(n):
        return (n % TM, 4 * y + 2 * (n // TM) + core)

    peers = [sibling]
    peers += [device("y", d) for d in ORDER]
    peers += [in_plane((plane + d) % 16) for d in range(1, 16)]
    barrier = pltpu.get_barrier_semaphore()
    for peer in peers:
        pl.semaphore_signal(barrier, inc=1, device_id=peer, device_id_type=MESH)

    raw[:, :N] = jnp.zeros((GROUP, N), jnp.float32)
    build_band(taps_ref, band)
    picker = build_picker(index_ref)
    b_hi, b_lo = split(band[...])
    both = jnp.concatenate([b_hi, b_lo], axis=1)
    load.wait()

    def finish(half, block, value):
        for j in range(TM):
            dec[j, half * HB + block] = value[8 * j : 8 * j + 8]
        picked = mm(picker, jnp.concatenate(split(value), axis=0))
        for j in range(NSRC // 8):
            pick[half, j, block] = picked[8 * j : 8 * j + 8]

    hi, lo = split(raw[:, 4 * N * BLOCKS :])
    wide = mm(hi, both[:N])
    finish(1, HB, wide[:, :N] + wide[:, N:] + mm(lo, b_hi[:N]))
    for j in range(NSRC // 8):
        pick[0, j, HB] = jnp.zeros((8, N), jnp.float32)

    def filter_half(half):
        for b0 in range(0, HB, 4):
            his, los = [], []
            for b in range(b0, b0 + 4):
                start = pl.multiple_of((half * HB + b) * (4 * N), 4 * N)
                hi, lo = split(raw[:, pl.ds(start, BAND)])
                his.append(hi)
                los.append(lo)
            hi, lo = jnp.concatenate(his, axis=0), jnp.concatenate(los, axis=0)
            wide = mm(hi, both)
            value = wide[:, :N] + wide[:, N:] + mm(lo, b_hi)
            for b in range(b0, b0 + 4):
                finish(half, b, value[GROUP * (b - b0) : GROUP * (b - b0 + 1)])

    started = []

    filter_half(1 - core)
    pl.semaphore_wait(barrier, len(peers))
    give = remote(pick.at[1 - core], pick_in, pick_sem.at[0], pick_sem.at[1], sibling)
    give.start()
    filter_half(core)
    own_blocks = pltpu.make_async_copy(dec.at[tm], chan_in.at[tm], own_sem.at[0])
    own_blocks.start()

    blocks = []
    for d in (1, 3, 2, 4, 5, 7, 6):
        other = (tm + d) % TM
        copy = remote(dec.at[other], chan_in.at[tm], dec_send.at[d], dec_recv.at[d], (other, ch))
        copy.start()
        blocks.append(copy)
    give.wait_recv()
    total[...] = pick[core] + pick_in[...]
    sums = []
    for d in ORDER:
        copy = remote(
            total.at[pl.ds(2 * ((y + d) % 4), 2)], rs_in.at[d], rs_send.at[d], rs_recv.at[d], device("y", d)
        )
        copy.start()
        sums.append(copy)
    for copy in sums:
        copy.wait_recv()
    acc[...] = (total[pl.ds(2 * y, 2)] + rs_in[1] + rs_in[2] + rs_in[3]).reshape(2 * PART * 8, N)
    for n in range(16):
        row_buf[n, :PART] = acc[pl.ds((n // TM) * PART * 8 + n % TM, PART, stride=8), :]
        row_buf[n, PART:] = jnp.zeros((16 - PART, N), jnp.float32)
    rows = []
    for d in range(1, 16):
        other = (plane + d) % 16
        copy = remote(row_buf.at[other], rows_in.at[zl, tm], row_send.at[d], row_recv.at[d], in_plane(other))
        copy.start()
        rows.append(copy)
    rows_in[zl, tm] = row_buf[plane]
    for copy in loads:
        copy.wait()
    for copy in rows:
        copy.wait_recv()
    halves[core] = rows_in[0] + rows_in[1]
    swap = remote(halves.at[core], halves.at[core], pick_sem.at[2], pick_sem.at[3], sibling)
    swap.start()
    swap.wait_recv()
    place = lax.broadcasted_iota(jnp.int32, (HB, N), 0)
    pieces = []
    for j in range(TM):
        early = halves[0, j, :HB]
        if j > 0:
            early = early + jnp.where(place == 0, halves[1, j - 1, HB : HB + 1], 0.0)
        pieces += [early, halves[1, j, :HB]]
    src_all[0, 0, 0] = whiten_series([jnp.concatenate(pieces, axis=0)], first, second, third, last, turn)[0]

    REST = pl.ds(1, 3)

    def region(kind, offsets):
        start, size, order = KINDS[kind]
        at = dict(zip(order, offsets))
        return src_all.at[at["y"], at["z"], at["x"], pl.ds(core * HALF + start, size)]

    counts = [{}, {}]

    def number(which, key):
        return counts[which].setdefault(key, len(counts[which]))

    def placed(offsets, axis, d):
        return tuple((4 - d) if i == axis else o for i, o in enumerate(offsets))

    def tag(offsets):
        return tuple("*" if not isinstance(o, int) else o for o in offsets)

    def send_on(kind, offsets, axis):
        for d in ORDER:
            to = placed(offsets, axis, d)
            n = number(0, (kind, tag(to), axis))
            copy = remote(
                region(kind, offsets), region(kind, to), g_send.at[n], g_recv.at[n], device(KINDS[kind][2][axis], d)
            )
            copy.start()
            started.append(copy)

    def arrived(kind, offsets, axis, ds=ORDER):
        for d in ds:
            to = placed(offsets, axis, d)
            n = number(0, (kind, tag(to), axis))
            part = region(kind, to)
            remote(part, part, g_send.at[n], g_recv.at[n], sibling).wait_recv()

    def share(kind, offsets):
        part = region(kind, offsets)
        n = number(1, (kind, tag(offsets)))
        copy = remote(part, part, f_send.at[n], f_recv.at[n], sibling)
        copy.start()
        started.append(copy)
        shared.append(copy)

    def settle():
        for copy in shared:
            copy.wait_recv()
        shared.clear()

    shared = []
    kinds = range(3)
    for axis in range(3):
        for kind in kinds:
            send_on(kind, (0, 0, 0), axis)

    place = lax.broadcasted_iota(jnp.int32, (BLOCKS, N), 0)

    def channel(c):
        pieces = []
        for j in range(TM):
            value = chan_in[j, :BLOCKS, c, :]
            if j > 0:
                value = value + jnp.where(place == 0, chan_in[j - 1, BLOCKS, c : c + 1, :], 0.0)
            pieces.append(value)
        return jnp.concatenate(pieces, axis=0)

    def channels(c0):
        whites = whiten_series([channel(c) for c in range(c0, c0 + 4)], first, second, third, last, turn)
        data = [jnp.concatenate([w, pltpu.roll(w, N - 1, 1)], axis=0) for w in whites]
        res = mm3((win[0], win[1]), split(jnp.concatenate(data, axis=1)))
        for i in range(2 * N // 8):
            for c in range(4):
                at = 8 * (c0 + c)
                spec_c[i, at : at + 8] = res[8 * i : 8 * i + 8, N * c : N * (c + 1)]

    def channel_slots(i, carry):
        for k in range(8):
            re = spec_c[i, pl.ds(k, 8, stride=8), :]
            im = spec_c[i + N // 8, pl.ds(k, 8, stride=8), :]
            straight, crossed = (re, im), (im, -re)
            if k == 0:
                single = jnp.broadcast_to(i == 0, re.shape)
                straight = (re, jnp.where(single, 0.0, im))
                crossed = (jnp.where(single, 0.0, im), jnp.where(single, im, -re))
            whole = []
            for halves in (straight, crossed):
                for r in range(-LAG_ROWS // 2, LAG_ROWS // 2):
                    moved = [h if r == 0 else pltpu.roll(h, -r % N, 1) for h in halves]
                    whole.append(jnp.concatenate(moved, axis=1))
            hi, lo = split(jnp.concatenate(whole, axis=0))
            chan_op[i * 8 + k] = jnp.concatenate([hi, lo], axis=0)
        return carry

    for kind in kinds:
        arrived(kind, (0, 0, 0), 0)
        send_on(kind, (REST, 0, 0), 1)
    for kind in kinds:
        arrived(kind, (0, 0, 0), 1)
        send_on(kind, (REST, 0, 0), 2)
        send_on(kind, (0, REST, 0), 2)
    for kind in kinds:
        arrived(kind, (0, 0, 0), 2)
        share(kind, (REST, 0, 0))
        share(kind, (0, REST, 0))
        share(kind, (0, 0, REST))
    own_blocks.wait()
    for copy in blocks:
        copy.wait_recv()
    channels(0)
    for kind in kinds:
        arrived(kind, (REST, 0, 0), 1)
        send_on(kind, (REST, REST, 0), 2)
    for kind in kinds:
        share(kind, (REST, REST, 0))
    channels(4)
    lax.fori_loop(0, N // 8, channel_slots, 0)
    for kind in kinds:
        arrived(kind, (REST, 0, 0), 2)
        share(kind, (REST, 0, REST))
        arrived(kind, (0, REST, 0), 2)
        share(kind, (0, REST, REST))
    settle()

    w_hi, w_lo = win[0][:, :N], win[1][:, :N]
    w_both = jnp.concatenate([w_hi, w_hi], axis=1)

    def transform(places):
        hi, lo = split(jnp.concatenate([src_all[ry, rz, rx] for ry, rz, rx in places], axis=1))
        rows = []
        for ry, rz, rx in places:
            z_s = (z + rz) % 4
            source = 8 * (2 * ((y + ry) % 4) + z_s % 2) + 4 * (z_s // 2) + (x + rx) % 4
            rows.append(pl.ds(pl.multiple_of(source * 8, 8), 8))
        res = mm(w_both, jnp.concatenate([hi, lo], axis=0)) + mm(w_lo, hi)
        for i in range(2 * N // 8):
            for e, at in enumerate(rows):
                spec[i, at, :] = res[8 * i : 8 * i + 8, N * e : N * (e + 1)]

    def column(ry, carry):
        transform([(ry, rz, 0) for rz in range(4)])
        return carry

    def early(t, carry):
        ry = jnp.where(t < 4, t, 0)
        rz = jnp.where(t < 4, 0, t - 3)
        transform([(ry, rz, rx) for rx in range(1, 4)])
        return carry

    lax.fori_loop(0, 4, column, 0)
    lax.fori_loop(0, 7, early, 0)

    left = lax.broadcasted_iota(jnp.int32, (NSRC, N), 1) < HALF

    def slots(i, carry):
        for k in range(UNROLL):
            n = i * UNROLL + k
            tile = i * (UNROLL // 8) + k // 8
            re = spec[tile, pl.ds(k % 8, NSRC, stride=8), :]
            im = spec[tile + N // 8, pl.ds(k % 8, NSRC, stride=8), :]
            hi, lo = split(jnp.concatenate([re, im], axis=1))
            res = lax.dot_general(
                chan_op[n],
                jnp.concatenate([hi, lo], axis=0),
                (((1,), (1,)), ((), ())),
                preferred_element_type=jnp.float32,
            )
            u = res[:64] + jnp.where(left, res[64:], 0.0)
            v = u + pltpu.roll(u, HALF, 1)
            prod[:, n] = jnp.where(left[:32], v[:32], v[32:]).reshape(LAG_ROWS, 8, N)
        part = pl.ds(i * UNROLL, UNROLL)
        pltpu.make_async_copy(prod.at[:, part], out_hbm.at[:, part], out_sem.at[i]).start()
        return carry

    for d in ORDER:
        for kind in kinds:
            arrived(kind, (REST, REST, 0), 2, (d,))
            share(kind, (REST, REST, 4 - d))
    settle()
    for ry in (1, 2, 3):
        transform([(ry, rz, rx) for rz in (1, 2, 3) for rx in (1, 2, 3)])
    lax.fori_loop(0, N // UNROLL, slots, 0)

    for i in range(N // UNROLL):
        part = pl.ds(i * UNROLL, UNROLL)
        pltpu.make_async_copy(prod.at[:, part], out_hbm.at[:, part], out_sem.at[i]).wait()
    swap.wait_send()
    give.wait_send()
    for copy in sums + rows + blocks + started:
        copy.wait_send()


def lags_kernel(prod_hbm, back_hbm, out_hbm, prod, back, out, in_sem, out_sem):
    table = pltpu.make_async_copy(back_hbm, back, in_sem.at[LAG_ROWS])
    table.start()
    loads = [pltpu.make_async_copy(prod_hbm.at[r], prod.at[r], in_sem.at[r]) for r in range(LAG_ROWS)]
    for copy in loads:
        copy.start()
    table.wait()
    k_hi = back[0]
    k_both = jnp.concatenate([back[0], back[1]], axis=1)
    for r in range(LAG_ROWS):
        loads[r].wait()
        for c0 in range(0, 8, 4):
            turned = [prod[r, :, c0 + c, :].T for c in range(4)]
            hi, lo = split(jnp.concatenate([jnp.concatenate([t[:NSRC], t[NSRC:]], axis=1) for t in turned], axis=0))
            wide = mm(hi, k_both)
            value = wide[:, :N] + wide[:, N:] + mm(lo, k_hi)
            out[c0 : c0 + 4, :, N * r : N * (r + 1)] = value.reshape(4, NSRC, N)
            if r == LAG_ROWS - 1:
                part = pl.ds(c0, 4)
                pltpu.make_async_copy(out.at[part], out_hbm.at[part], out_sem.at[c0 // 4]).start()
    for c0 in range(0, 8, 4):
        part = pl.ds(c0, 4)
        pltpu.make_async_copy(out.at[part], out_hbm.at[part], out_sem.at[c0 // 4]).wait()


def on_device(strain, fir_taps, source_index):
    tables = series_tables()
    win, back = window_tables()
    tables = [stack_np(t) for t in tables[:4]] + [tables[4], stack_np(win)]
    dma = pltpu.SemaphoreType.DMA
    f32 = jnp.float32
    smem = pl.BlockSpec(memory_space=pltpu.SMEM)
    anywhere = pl.BlockSpec(memory_space=pl.ANY)
    products = pl.pallas_call(
        kernel,
        out_shape=jax.ShapeDtypeStruct((LAG_ROWS, N, 8, N), f32),
        in_specs=[anywhere, smem, smem] + [anywhere] * len(tables),
        out_specs=anywhere,
        scratch_shapes=[
            VMEM((GROUP, N + 4 * N * BLOCKS), f32),
            VMEM((BAND, N), f32),
            VMEM((TM, BLOCKS + 1, 8, N), f32),
            VMEM((2, 8, PART, 8, N), f32),
            VMEM((8, PART, 8, N), f32),
            VMEM((8, PART, 8, N), f32),
            VMEM((4, 2, PART, 8, N), f32),
            VMEM((2 * PART * 8, N), f32),
            VMEM((16, 16, N), f32),
            VMEM((2, TM, 16, N), f32),
            VMEM((2, TM, 16, N), f32),
            VMEM((TM, BLOCKS + 1, 8, N), f32),
            VMEM((4, 4, 4, N, N), f32),
            VMEM((2 * N // 8, 64, N), f32),
            VMEM((N, N, 2 * N), jnp.bfloat16),
            VMEM((2 * N // 8, 8 * NSRC, N), f32),
            VMEM((LAG_ROWS, N, 8, N), f32),
        ]
        + [VMEM(t.shape, jnp.dtype(t.dtype)) for t in tables]
        + [
            dma((1 + len(tables),)),
            dma((2,)),
            dma((4,)),
            dma((TM,)),
            dma((TM,)),
            dma((4,)),
            dma((4,)),
            dma((16,)),
            dma((16,)),
        ]
        + [dma((81,))] * 2
        + [dma((27,))] * 2
        + [dma((N // UNROLL,))],
        compiler_params=pltpu.CompilerParams(
            collective_id=0, has_side_effects=True, vmem_limit_bytes=VMEM_LIMIT
        ),
        name="interferometry",
    )(strain, fir_taps, source_index, *tables)
    return pl.pallas_call(
        lags_kernel,
        out_shape=jax.ShapeDtypeStruct((8, NSRC, LAG_ROWS * N), f32),
        in_specs=[anywhere, anywhere],
        out_specs=anywhere,
        scratch_shapes=[
            VMEM((LAG_ROWS, N, 8, N), f32),
            VMEM((2, 2 * N, N), jnp.bfloat16),
            VMEM((8, NSRC, LAG_ROWS * N), f32),
            dma((LAG_ROWS + 1,)),
            dma((2,)),
        ],
        compiler_params=pltpu.CompilerParams(vmem_limit_bytes=VMEM_LIMIT),
        name="lags",
    )(products, stack_np(back))


def solution(mesh):
    return jax.shard_map(
        on_device,
        mesh=mesh,
        in_specs=(P("chan", "tm"), P(), P()),
        out_specs=P(("chan", "tm"), None, None),
        check_vma=False,
    )
```

```python
import functools

import jax
import jax.numpy as jnp
import ml_dtypes
import numpy as np
from jax import lax
from jax.experimental import pallas as pl
from jax.experimental.pallas import tpu as pltpu
from jax.sharding import PartitionSpec as P

MESH = pl.DeviceIdType.MESH
VMEM = pltpu.VMEM
N = 128
NT = N * N
HALF = N // 2
TAPS = 64
NSRC = 64
FLOOR = 0.1
LAG_ROWS = 4
GROUP = 64
TM = 8
BLOCKS = 16
BAND = 5 * N
HB = BLOCKS // 2
PART = HB + 1
KINDS = ((0, 24, "xyz"), (24, 16, "yzx"), (40, 24, "zxy"))
ORDER = (1, 3, 2)
UNROLL = 64
VMEM_LIMIT = 56 * 1024 * 1024


def split_np(table):
    high = table.astype(np.float32).astype(ml_dtypes.bfloat16)
    low = (table - high.astype(np.float64)).astype(np.float32).astype(ml_dtypes.bfloat16)
    return high, low


def stack_np(table):
    return np.stack(split_np(table))


def series_tables():
    k = np.arange(HALF)[:, None]
    q = np.arange(N)[None, :]
    ang = 2 * np.pi * ((k * q) % N) / N
    first = np.concatenate([np.cos(ang), -np.sin(ang)])
    first[HALF] = np.cos(np.pi * np.arange(N))
    ang = 2 * np.pi * ((np.arange(N)[:, None] * np.arange(N)[None, :]) % N) / N
    c, s = np.cos(ang), np.sin(ang)
    second = np.block([[c, -s], [s, c]])
    third = np.block([[c, s], [-s, c]])
    ang = 2 * np.pi * ((np.arange(N)[:, None] * np.arange(HALF)[None, :]) % N) / N
    last = np.concatenate([2 * np.cos(ang), -2 * np.sin(ang)], axis=1) / N
    last[:, 0] = 1.0 / N
    last[:, HALF] = np.cos(np.pi * np.arange(N)) / N
    ang = 2 * np.pi * (np.arange(HALF + 8)[:, None] * np.arange(N)[None, :]) / NT
    turn = np.stack([np.cos(ang), np.sin(ang)]).astype(np.float32)
    return first, second, third, last, turn


def window_tables():
    f = np.arange(N)[:, None]
    u = np.arange(2 * N)[None, :]
    ang = 2 * np.pi * ((f * u) % (2 * N)) / (2 * N)
    win = np.concatenate([np.cos(ang), -np.sin(ang)])
    win[N] = np.cos(np.pi * np.arange(2 * N))
    m = np.arange(N)[None, :]
    ang = 2 * np.pi * ((f * m) % (2 * N)) / (2 * N)
    scale = 1.0 / (2 * N * N)
    back = np.concatenate([2 * np.cos(ang), -2 * np.sin(ang)]) * scale
    back[0] = scale
    back[N] = np.cos(np.pi * np.arange(N)) * scale
    return win, back


def split(value):
    high = value.astype(jnp.bfloat16)
    low = (value - high.astype(jnp.float32)).astype(jnp.bfloat16)
    return high, low


def mm(a, b):
    return jnp.dot(a, b, preferred_element_type=jnp.float32)


def mm3(a, b):
    return mm(a[0], b[0]) + mm(a[0], b[1]) + mm(a[1], b[0])


def whiten_series(series, first, second, third, last, turn):
    count = len(series)
    powers = [jnp.sum(x * x) for x in series]
    x_hi, x_lo = split(jnp.concatenate(series, axis=1))
    a_hi, a_lo = first[0], first[1]
    part = mm(jnp.concatenate([a_hi, a_hi], axis=1), jnp.concatenate([x_hi, x_lo], axis=0)) + mm(a_lo, x_hi)
    cos, sin = turn[0, :HALF], turn[1, :HALF]
    cos_mid, sin_mid = turn[0, HALF : HALF + 1], turn[1, HALF : HALF + 1]
    top = lax.broadcasted_iota(jnp.int32, (HALF, N), 0) == 0
    cos_im = jnp.where(top, 0.0, cos)
    rows, mids = [], []
    for i in range(count):
        re = part[:HALF, N * i : N * (i + 1)]
        im = part[HALF:, N * i : N * (i + 1)]
        rows.append(jnp.concatenate([re * cos + im * sin, im * cos_im - re * sin], axis=1))
        mid = im[:1]
        mids.append(jnp.concatenate([mid * cos_mid, -mid * sin_mid], axis=1))
    pad = -count % 8
    if pad:
        mids.append(jnp.zeros((pad, 2 * N), jnp.float32))
    turned = jnp.concatenate(rows + mids, axis=0)
    spec = mm3(split(turned), (second[0], second[1]))
    spec_re, spec_im = spec[:, :N], spec[:, N:]
    energy = spec_re * spec_re + spec_im * spec_im
    floor = [jnp.broadcast_to(FLOOR * p, (HALF, N)) for p in powers]
    floor += [jnp.broadcast_to(FLOOR * p, (1, N)) for p in powers]
    if pad:
        floor.append(jnp.ones((pad, N), jnp.float32))
    scale = lax.rsqrt(energy + jnp.concatenate(floor, axis=0))
    white = jnp.concatenate([spec_re * scale, spec_im * scale], axis=1)
    back = mm3(split(white), (third[0], third[1]))
    cols = []
    for i in range(count):
        re = back[HALF * i : HALF * (i + 1), :N]
        im = back[HALF * i : HALF * (i + 1), N:]
        mid = HALF * count + i
        mid_re, mid_im = back[mid : mid + 1, :N], back[mid : mid + 1, N:]
        out_re = re * cos - im * sin
        out_im = jnp.where(top, mid_re * cos_mid - mid_im * sin_mid, im * cos + re * sin)
        cols.append(jnp.concatenate([out_re, out_im], axis=0))
    y_hi, y_lo = split(jnp.concatenate(cols, axis=1))
    l_hi, l_lo = last[0], last[1]
    time = mm(jnp.concatenate([l_hi, l_hi], axis=1), jnp.concatenate([y_hi, y_lo], axis=0)) + mm(l_lo, y_hi)
    return [time[:, N * i : N * (i + 1)].T for i in range(count)]


def remote(src, dst, send, recv, device):
    return pltpu.make_async_remote_copy(
        src_ref=src, dst_ref=dst, send_sem=send, recv_sem=recv, device_id=device, device_id_type=MESH
    )


def build_band(taps_ref, band):
    rho = lax.broadcasted_iota(jnp.int32, (8, N), 0)
    lane = lax.broadcasted_iota(jnp.int32, (8, N), 1)
    shifted = 4 * lane - rho
    base = jnp.zeros((8, N), jnp.float32)
    for j in range(TAPS):
        base = jnp.where(shifted == j - 3, taps_ref[j], base)
    for t in range(BAND // 8):
        move = (2 * t - 32) % N
        tap = 4 * lane + (131 - 8 * t) - rho
        rolled = base if move == 0 else pltpu.roll(base, move, 1)
        band[8 * t : 8 * t + 8, :] = jnp.where((tap >= 0) & (tap < TAPS), rolled, 0.0)


def build_picker(index_ref):
    row = lax.broadcasted_iota(jnp.int32, (NSRC, 2 * GROUP), 0)
    wanted = jnp.zeros((NSRC, 2 * GROUP), jnp.int32)
    for s in range(NSRC):
        wanted = jnp.where(row == s, index_ref[s], wanted)
    owned = lax.broadcasted_iota(jnp.int32, (NSRC, 2 * GROUP), 1) % GROUP + lax.axis_index("chan") * GROUP
    return jnp.where(wanted == owned, 1.0, 0.0).astype(jnp.bfloat16)


def kernel(
    strain_hbm, taps_ref, index_ref, first_hbm, second_hbm, third_hbm, last_hbm, turn_hbm, win_hbm, out_hbm,
    raw, band, dec, pick, pick_in, total, rs_in, acc, row_buf, rows_in, halves, chan_in, src_all, spec_c, chan_op, spec, prod,
    first, second, third, last, turn, win,
    load_sem, own_sem, pick_sem, dec_send, dec_recv, rs_send, rs_recv, row_send, row_recv,
    g_send, g_recv, f_send, f_recv, out_sem,
):
    tm = lax.axis_index("tm")
    ch = lax.axis_index("chan")
    x, zh = tm % 4, tm // 4
    y, zl, core = ch // 4, (ch // 2) % 2, ch % 2
    z, pair = 2 * zh + zl, ch // 2

    tables = (
        (first_hbm, first), (second_hbm, second), (third_hbm, third), (last_hbm, last), (turn_hbm, turn),
        (win_hbm, win),
    )
    load = pltpu.make_async_copy(strain_hbm, raw.at[:, pl.ds(N, 4 * N * BLOCKS)], load_sem.at[0])
    load.start()
    loads = [pltpu.make_async_copy(a, b, load_sem.at[1 + i]) for i, (a, b) in enumerate(tables)]
    for copy in loads:
        copy.start()

    ring_x = [x] + [(x + d) % 4 for d in (1, 2, 3)]
    ring_y = [y] + [(y + d) % 4 for d in (1, 2, 3)]
    ring_z = [z] + [(z + d) % 4 for d in (1, 2, 3)]
    part_y = [16 * v for v in ring_y]
    part_z = [8 * (v % 2) + 4 * (v // 2) for v in ring_z]
    devices = {("x", d): (zh * 4 + ring_x[d], ch) for d in (1, 2, 3)}
    devices.update({("y", d): (tm, ring_y[d] * 4 + zl * 2 + core) for d in (1, 2, 3)})
    devices.update(
        {("z", d): ((ring_z[d] // 2) * 4 + x, y * 4 + (ring_z[d] % 2) * 2 + core) for d in (1, 2, 3)}
    )
    own_rows = core * HALF

    def device(axis, d):
        return devices[axis, d]

    sibling = (tm, 2 * pair + 1 - core)
    plane = 8 * zl + tm

    def in_plane(n):
        return (n % TM, 4 * y + 2 * (n // TM) + core)

    peers = [sibling]
    peers += [device("y", d) for d in ORDER]
    peers += [in_plane((plane + d) % 16) for d in range(1, 16)]
    barrier = pltpu.get_barrier_semaphore()
    for peer in peers:
        pl.semaphore_signal(barrier, inc=1, device_id=peer, device_id_type=MESH)

    raw[:, :N] = jnp.zeros((GROUP, N), jnp.float32)
    build_band(taps_ref, band)
    picker = build_picker(index_ref)
    b_hi, b_lo = split(band[...])
    both = jnp.concatenate([b_hi, b_lo], axis=1)
    load.wait()

    def finish(half, block, value):
        for j in range(TM):
            dec[j, half * HB + block] = value[8 * j : 8 * j + 8]
        picked = mm(picker, jnp.concatenate(split(value), axis=0))
        for j in range(NSRC // 8):
            pick[half, j, block] = picked[8 * j : 8 * j + 8]

    hi, lo = split(raw[:, 4 * N * BLOCKS :])
    wide = mm(hi, both[:N])
    finish(1, HB, wide[:, :N] + wide[:, N:] + mm(lo, b_hi[:N]))
    for j in range(NSRC // 8):
        pick[0, j, HB] = jnp.zeros((8, N), jnp.float32)

    def filter_half(half):
        for b0 in range(0, HB, 4):
            his, los = [], []
            for b in range(b0, b0 + 4):
                start = pl.multiple_of((half * HB + b) * (4 * N), 4 * N)
                hi, lo = split(raw[:, pl.ds(start, BAND)])
                his.append(hi)
                los.append(lo)
            hi, lo = jnp.concatenate(his, axis=0), jnp.concatenate(los, axis=0)
            wide = mm(hi, both)
            value = wide[:, :N] + wide[:, N:] + mm(lo, b_hi)
            for b in range(b0, b0 + 4):
                finish(half, b, value[GROUP * (b - b0) : GROUP * (b - b0 + 1)])

    started = []

    filter_half(1 - core)
    pl.semaphore_wait(barrier, len(peers))
    give = remote(pick.at[1 - core], pick_in, pick_sem.at[0], pick_sem.at[1], sibling)
    give.start()
    filter_half(core)
    own_blocks = pltpu.make_async_copy(dec.at[tm], chan_in.at[tm], own_sem.at[0])
    own_blocks.start()

    blocks = []
    for d in (1, 3, 2, 4, 5, 7, 6):
        other = (tm + d) % TM
        copy = remote(dec.at[other], chan_in.at[tm], dec_send.at[d], dec_recv.at[d], (other, ch))
        copy.start()
        blocks.append(copy)
    give.wait_recv()
    total[...] = pick[core] + pick_in[...]
    sums = []
    for d in ORDER:
        copy = remote(
            total.at[pl.ds(2 * ring_y[d], 2)], rs_in.at[d], rs_send.at[d], rs_recv.at[d], device("y", d)
        )
        copy.start()
        sums.append(copy)
    for copy in sums:
        copy.wait_recv()
    acc[...] = (total[pl.ds(2 * y, 2)] + rs_in[1] + rs_in[2] + rs_in[3]).reshape(2 * PART * 8, N)
    for n in range(16):
        row_buf[n, :PART] = acc[pl.ds((n // TM) * PART * 8 + n % TM, PART, stride=8), :]
        row_buf[n, PART:] = jnp.zeros((16 - PART, N), jnp.float32)
    rows = []
    for d in range(1, 16):
        other = (plane + d) % 16
        copy = remote(row_buf.at[other], rows_in.at[zl, tm], row_send.at[d], row_recv.at[d], in_plane(other))
        copy.start()
        rows.append(copy)
    rows_in[zl, tm] = row_buf[plane]
    for copy in loads:
        copy.wait()
    for copy in rows:
        copy.wait_recv()
    halves[core] = rows_in[0] + rows_in[1]
    swap = remote(halves.at[core], halves.at[core], pick_sem.at[2], pick_sem.at[3], sibling)
    swap.start()
    swap.wait_recv()
    place = lax.broadcasted_iota(jnp.int32, (HB, N), 0)
    pieces = []
    for j in range(TM):
        early = halves[0, j, :HB]
        if j > 0:
            early = early + jnp.where(place == 0, halves[1, j - 1, HB : HB + 1], 0.0)
        pieces += [early, halves[1, j, :HB]]
    src_all[0, 0, 0] = whiten_series([jnp.concatenate(pieces, axis=0)], first, second, third, last, turn)[0]

    REST = pl.ds(1, 3)

    def region(kind, offsets):
        start, size, order = KINDS[kind]
        at = dict(zip(order, offsets))
        return src_all.at[at["y"], at["z"], at["x"], pl.ds(own_rows + start, size)]

    counts = [{}, {}]

    def number(which, key):
        return counts[which].setdefault(key, len(counts[which]))

    def placed(offsets, axis, d):
        return tuple((4 - d) if i == axis else o for i, o in enumerate(offsets))

    def tag(offsets):
        return tuple("*" if not isinstance(o, int) else o for o in offsets)

    def send_on(kind, offsets, axis):
        for d in ORDER:
            to = placed(offsets, axis, d)
            n = number(0, (kind, tag(to), axis))
            copy = remote(
                region(kind, offsets), region(kind, to), g_send.at[n], g_recv.at[n], device(KINDS[kind][2][axis], d)
            )
            copy.start()
            started.append(copy)

    def arrived(kind, offsets, axis, ds=ORDER):
        for d in ds:
            to = placed(offsets, axis, d)
            n = number(0, (kind, tag(to), axis))
            part = region(kind, to)
            remote(part, part, g_send.at[n], g_recv.at[n], sibling).wait_recv()

    def share(kind, offsets):
        part = region(kind, offsets)
        n = number(1, (kind, tag(offsets)))
        copy = remote(part, part, f_send.at[n], f_recv.at[n], sibling)
        copy.start()
        started.append(copy)
        shared.append(copy)

    def settle():
        for copy in shared:
            copy.wait_recv()
        shared.clear()

    shared = []
    kinds = range(3)
    for axis in range(3):
        for kind in kinds:
            send_on(kind, (0, 0, 0), axis)

    place = lax.broadcasted_iota(jnp.int32, (BLOCKS, N), 0)

    def channel(c):
        pieces = []
        for j in range(TM):
            value = chan_in[j, :BLOCKS, c, :]
            if j > 0:
                value = value + jnp.where(place == 0, chan_in[j - 1, BLOCKS, c : c + 1, :], 0.0)
            pieces.append(value)
        return jnp.concatenate(pieces, axis=0)

    def channels(c0):
        whites = whiten_series([channel(c) for c in range(c0, c0 + 4)], first, second, third, last, turn)
        data = [jnp.concatenate([w, pltpu.roll(w, N - 1, 1)], axis=0) for w in whites]
        res = mm3((win[0], win[1]), split(jnp.concatenate(data, axis=1)))
        for i in range(2 * N // 8):
            for c in range(4):
                at = 8 * (c0 + c)
                spec_c[i, at : at + 8] = res[8 * i : 8 * i + 8, N * c : N * (c + 1)]

    def channel_slots(i, carry):
        for k in range(8):
            re = spec_c[i, pl.ds(k, 8, stride=8), :]
            im = spec_c[i + N // 8, pl.ds(k, 8, stride=8), :]
            straight, crossed = (re, im), (im, -re)
            if k == 0:
                single = jnp.broadcast_to(i == 0, re.shape)
                straight = (re, jnp.where(single, 0.0, im))
                crossed = (jnp.where(single, 0.0, im), jnp.where(single, im, -re))
            whole = []
            for halves in (straight, crossed):
                for r in range(-LAG_ROWS // 2, LAG_ROWS // 2):
                    moved = [h if r == 0 else pltpu.roll(h, -r % N, 1) for h in halves]
                    whole.append(jnp.concatenate(moved, axis=1))
            hi, lo = split(jnp.concatenate(whole, axis=0))
            chan_op[i * 8 + k] = jnp.concatenate([hi, lo], axis=0)
        return carry

    for kind in kinds:
        arrived(kind, (0, 0, 0), 0)
        send_on(kind, (REST, 0, 0), 1)
    for kind in kinds:
        arrived(kind, (0, 0, 0), 1)
        send_on(kind, (REST, 0, 0), 2)
        send_on(kind, (0, REST, 0), 2)
    for kind in kinds:
        arrived(kind, (0, 0, 0), 2)
        share(kind, (REST, 0, 0))
        share(kind, (0, REST, 0))
        share(kind, (0, 0, REST))
    own_blocks.wait()
    for copy in blocks:
        copy.wait_recv()
    channels(0)
    for kind in kinds:
        arrived(kind, (REST, 0, 0), 1)
        send_on(kind, (REST, REST, 0), 2)
    for kind in kinds:
        share(kind, (REST, REST, 0))
    channels(4)
    lax.fori_loop(0, N // 8, channel_slots, 0)
    for kind in kinds:
        arrived(kind, (REST, 0, 0), 2)
        share(kind, (REST, 0, REST))
        arrived(kind, (0, REST, 0), 2)
        share(kind, (0, REST, REST))
    settle()

    w_hi, w_lo = win[0][:, :N], win[1][:, :N]
    w_both = jnp.concatenate([w_hi, w_hi], axis=1)

    def transform(places):
        hi, lo = split(jnp.concatenate([src_all[ry, rz, rx] for ry, rz, rx in places], axis=1))
        rows = []
        for ry, rz, rx in places:
            source = part_y[ry] + part_z[rz] + ring_x[rx]
            rows.append(pl.ds(pl.multiple_of(source * 8, 8), 8))
        res = mm(w_both, jnp.concatenate([hi, lo], axis=0)) + mm(w_lo, hi)
        for i in range(2 * N // 8):
            for e, at in enumerate(rows):
                spec[i, at, :] = res[8 * i : 8 * i + 8, N * e : N * (e + 1)]

    def hand_over(d):
        for kind in kinds:
            arrived(kind, (REST, REST, 0), 2, (d,))
            share(kind, (REST, REST, 4 - d))

    near = [(ry, rz, 0) for ry in range(4) for rz in range(4)]
    near += [(ry, rz, rx) for ry, rz in ((0, 0), (1, 0), (2, 0), (3, 0), (0, 1), (0, 2), (0, 3)) for rx in (1, 2, 3)]
    transform(near[:8])
    transform(near[8:16])
    hand_over(1)
    hand_over(3)
    transform(near[16:23])
    transform(near[23:30])
    transform(near[30:])
    hand_over(2)
    settle()
    for ry in (1, 2, 3):
        transform([(ry, rz, rx) for rz in (1, 2, 3) for rx in (1, 2, 3)])

    left = lax.broadcasted_iota(jnp.int32, (NSRC, N), 1) < HALF

    def slots(i, carry):
        for k in range(UNROLL):
            n = i * UNROLL + k
            tile = i * (UNROLL // 8) + k // 8
            re = spec[tile, pl.ds(k % 8, NSRC, stride=8), :]
            im = spec[tile + N // 8, pl.ds(k % 8, NSRC, stride=8), :]
            hi, lo = split(jnp.concatenate([re, im], axis=1))
            res = lax.dot_general(
                chan_op[n],
                jnp.concatenate([hi, lo], axis=0),
                (((1,), (1,)), ((), ())),
                preferred_element_type=jnp.float32,
            )
            u = res[:64] + jnp.where(left, res[64:], 0.0)
            v = u + pltpu.roll(u, HALF, 1)
            prod[:, n] = jnp.where(left[:32], v[:32], v[32:]).reshape(LAG_ROWS, 8, N)
        part = pl.ds(i * UNROLL, UNROLL)
        pltpu.make_async_copy(prod.at[:, part], out_hbm.at[:, part], out_sem.at[i]).start()
        return carry

    lax.fori_loop(0, N // UNROLL, slots, 0)

    for i in range(N // UNROLL):
        part = pl.ds(i * UNROLL, UNROLL)
        pltpu.make_async_copy(prod.at[:, part], out_hbm.at[:, part], out_sem.at[i]).wait()
    swap.wait_send()
    give.wait_send()
    for copy in sums + rows + blocks + started:
        copy.wait_send()


def lags_kernel(prod_hbm, back_hbm, out_hbm, prod, back, out, in_sem, out_sem):
    table = pltpu.make_async_copy(back_hbm, back, in_sem.at[LAG_ROWS])
    table.start()
    loads = [pltpu.make_async_copy(prod_hbm.at[r], prod.at[r], in_sem.at[r]) for r in range(LAG_ROWS)]
    for copy in loads:
        copy.start()
    table.wait()
    k_hi = back[0]
    k_both = jnp.concatenate([back[0], back[1]], axis=1)
    for r in range(LAG_ROWS):
        loads[r].wait()
        for c0 in range(0, 8, 4):
            turned = [prod[r, :, c0 + c, :].T for c in range(4)]
            hi, lo = split(jnp.concatenate([jnp.concatenate([t[:NSRC], t[NSRC:]], axis=1) for t in turned], axis=0))
            wide = mm(hi, k_both)
            value = wide[:, :N] + wide[:, N:] + mm(lo, k_hi)
            out[c0 : c0 + 4, :, N * r : N * (r + 1)] = value.reshape(4, NSRC, N)
            if r == LAG_ROWS - 1:
                part = pl.ds(c0, 4)
                pltpu.make_async_copy(out.at[part], out_hbm.at[part], out_sem.at[c0 // 4]).start()
    for c0 in range(0, 8, 4):
        part = pl.ds(c0, 4)
        pltpu.make_async_copy(out.at[part], out_hbm.at[part], out_sem.at[c0 // 4]).wait()


def on_device(strain, fir_taps, source_index):
    tables = series_tables()
    win, back = window_tables()
    tables = [stack_np(t) for t in tables[:4]] + [tables[4], stack_np(win)]
    dma = pltpu.SemaphoreType.DMA
    f32 = jnp.float32
    smem = pl.BlockSpec(memory_space=pltpu.SMEM)
    anywhere = pl.BlockSpec(memory_space=pl.ANY)
    products = pl.pallas_call(
        kernel,
        out_shape=jax.ShapeDtypeStruct((LAG_ROWS, N, 8, N), f32),
        in_specs=[anywhere, smem, smem] + [anywhere] * len(tables),
        out_specs=anywhere,
        scratch_shapes=[
            VMEM((GROUP, N + 4 * N * BLOCKS), f32),
            VMEM((BAND, N), f32),
            VMEM((TM, BLOCKS + 1, 8, N), f32),
            VMEM((2, 8, PART, 8, N), f32),
            VMEM((8, PART, 8, N), f32),
            VMEM((8, PART, 8, N), f32),
            VMEM((4, 2, PART, 8, N), f32),
            VMEM((2 * PART * 8, N), f32),
            VMEM((16, 16, N), f32),
            VMEM((2, TM, 16, N), f32),
            VMEM((2, TM, 16, N), f32),
            VMEM((TM, BLOCKS + 1, 8, N), f32),
            VMEM((4, 4, 4, N, N), f32),
            VMEM((2 * N // 8, 64, N), f32),
            VMEM((N, N, 2 * N), jnp.bfloat16),
            VMEM((2 * N // 8, 8 * NSRC, N), f32),
            VMEM((LAG_ROWS, N, 8, N), f32),
        ]
        + [VMEM(t.shape, jnp.dtype(t.dtype)) for t in tables]
        + [
            dma((1 + len(tables),)),
            dma((2,)),
            dma((4,)),
            dma((TM,)),
            dma((TM,)),
            dma((4,)),
            dma((4,)),
            dma((16,)),
            dma((16,)),
        ]
        + [dma((81,))] * 2
        + [dma((27,))] * 2
        + [dma((N // UNROLL,))],
        compiler_params=pltpu.CompilerParams(
            collective_id=0, has_side_effects=True, vmem_limit_bytes=VMEM_LIMIT
        ),
        name="interferometry",
    )(strain, fir_taps, source_index, *tables)
    return pl.pallas_call(
        lags_kernel,
        out_shape=jax.ShapeDtypeStruct((8, NSRC, LAG_ROWS * N), f32),
        in_specs=[anywhere, anywhere],
        out_specs=anywhere,
        scratch_shapes=[
            VMEM((LAG_ROWS, N, 8, N), f32),
            VMEM((2, 2 * N, N), jnp.bfloat16),
            VMEM((8, NSRC, LAG_ROWS * N), f32),
            dma((LAG_ROWS + 1,)),
            dma((2,)),
        ],
        compiler_params=pltpu.CompilerParams(vmem_limit_bytes=VMEM_LIMIT),
        name="lags",
    )(products, stack_np(back))


def solution(mesh):
    return jax.shard_map(
        on_device,
        mesh=mesh,
        in_specs=(P("chan", "tm"), P(), P()),
        out_specs=P(("chan", "tm"), None, None),
        check_vma=False,
    )
```

```python
import functools

import jax
import jax.numpy as jnp
import ml_dtypes
import numpy as np
from jax import lax
from jax.experimental import pallas as pl
from jax.experimental.pallas import tpu as pltpu
from jax.sharding import PartitionSpec as P

MESH = pl.DeviceIdType.MESH
VMEM = pltpu.VMEM
N = 128
NT = N * N
HALF = N // 2
TAPS = 64
NSRC = 64
FLOOR = 0.1
LAG_ROWS = 4
GROUP = 64
TM = 8
BLOCKS = 16
BAND = 5 * N
HB = BLOCKS // 2
PART = HB + 1
KINDS = ((0, 24, "xyz"), (24, 16, "yzx"), (40, 24, "zxy"))
ORDER = (1, 3, 2)
UNROLL = 64
VMEM_LIMIT = 56 * 1024 * 1024


def split_np(table):
    high = table.astype(np.float32).astype(ml_dtypes.bfloat16)
    low = (table - high.astype(np.float64)).astype(np.float32).astype(ml_dtypes.bfloat16)
    return high, low


def stack_np(table):
    return np.stack(split_np(table))


def series_tables():
    k = np.arange(HALF)[:, None]
    q = np.arange(N)[None, :]
    ang = 2 * np.pi * ((k * q) % N) / N
    first = np.concatenate([np.cos(ang), -np.sin(ang)])
    first[HALF] = np.cos(np.pi * np.arange(N))
    ang = 2 * np.pi * ((np.arange(N)[:, None] * np.arange(N)[None, :]) % N) / N
    c, s = np.cos(ang), np.sin(ang)
    second = np.block([[c, -s], [s, c]])
    third = np.block([[c, s], [-s, c]])
    ang = 2 * np.pi * ((np.arange(N)[:, None] * np.arange(HALF)[None, :]) % N) / N
    last = np.concatenate([2 * np.cos(ang), -2 * np.sin(ang)], axis=1) / N
    last[:, 0] = 1.0 / N
    last[:, HALF] = np.cos(np.pi * np.arange(N)) / N
    ang = 2 * np.pi * (np.arange(HALF + 8)[:, None] * np.arange(N)[None, :]) / NT
    turn = np.stack([np.cos(ang), np.sin(ang)]).astype(np.float32)
    return first, second, third, last, turn


def window_tables():
    f = np.arange(N)[:, None]
    u = np.arange(2 * N)[None, :]
    ang = 2 * np.pi * ((f * u) % (2 * N)) / (2 * N)
    win = np.concatenate([np.cos(ang), -np.sin(ang)])
    win[N] = np.cos(np.pi * np.arange(2 * N))
    m = np.arange(N)[None, :]
    ang = 2 * np.pi * ((f * m) % (2 * N)) / (2 * N)
    scale = 1.0 / (2 * N * N)
    back = np.concatenate([2 * np.cos(ang), -2 * np.sin(ang)]) * scale
    back[0] = scale
    back[N] = np.cos(np.pi * np.arange(N)) * scale
    return win, back


def split(value):
    high = value.astype(jnp.bfloat16)
    low = (value - high.astype(jnp.float32)).astype(jnp.bfloat16)
    return high, low


def mm(a, b):
    return jnp.dot(a, b, preferred_element_type=jnp.float32)


def mm3(a, b):
    return mm(a[0], b[0]) + mm(a[0], b[1]) + mm(a[1], b[0])


def whiten_series(series, first, second, third, last, turn):
    count = len(series)
    powers = [jnp.sum(x * x) for x in series]
    x_hi, x_lo = split(jnp.concatenate(series, axis=1))
    a_hi, a_lo = first[0], first[1]
    part = mm(jnp.concatenate([a_hi, a_hi], axis=1), jnp.concatenate([x_hi, x_lo], axis=0)) + mm(a_lo, x_hi)
    cos, sin = turn[0, :HALF], turn[1, :HALF]
    cos_mid, sin_mid = turn[0, HALF : HALF + 1], turn[1, HALF : HALF + 1]
    top = lax.broadcasted_iota(jnp.int32, (HALF, N), 0) == 0
    cos_im = jnp.where(top, 0.0, cos)
    rows, mids = [], []
    for i in range(count):
        re = part[:HALF, N * i : N * (i + 1)]
        im = part[HALF:, N * i : N * (i + 1)]
        rows.append(jnp.concatenate([re * cos + im * sin, im * cos_im - re * sin], axis=1))
        mid = im[:1]
        mids.append(jnp.concatenate([mid * cos_mid, -mid * sin_mid], axis=1))
    pad = -count % 8
    if pad:
        mids.append(jnp.zeros((pad, 2 * N), jnp.float32))
    turned = jnp.concatenate(rows + mids, axis=0)
    spec = mm3(split(turned), (second[0], second[1]))
    spec_re, spec_im = spec[:, :N], spec[:, N:]
    energy = spec_re * spec_re + spec_im * spec_im
    floor = [jnp.broadcast_to(FLOOR * p, (HALF, N)) for p in powers]
    floor += [jnp.broadcast_to(FLOOR * p, (1, N)) for p in powers]
    if pad:
        floor.append(jnp.ones((pad, N), jnp.float32))
    scale = lax.rsqrt(energy + jnp.concatenate(floor, axis=0))
    white = jnp.concatenate([spec_re * scale, spec_im * scale], axis=1)
    back = mm3(split(white), (third[0], third[1]))
    cols = []
    for i in range(count):
        re = back[HALF * i : HALF * (i + 1), :N]
        im = back[HALF * i : HALF * (i + 1), N:]
        mid = HALF * count + i
        mid_re, mid_im = back[mid : mid + 1, :N], back[mid : mid + 1, N:]
        out_re = re * cos - im * sin
        out_im = jnp.where(top, mid_re * cos_mid - mid_im * sin_mid, im * cos + re * sin)
        cols.append(jnp.concatenate([out_re, out_im], axis=0))
    y_hi, y_lo = split(jnp.concatenate(cols, axis=1))
    l_hi, l_lo = last[0], last[1]
    time = mm(jnp.concatenate([l_hi, l_hi], axis=1), jnp.concatenate([y_hi, y_lo], axis=0)) + mm(l_lo, y_hi)
    return [time[:, N * i : N * (i + 1)].T for i in range(count)]


def remote(src, dst, send, recv, device):
    return pltpu.make_async_remote_copy(
        src_ref=src, dst_ref=dst, send_sem=send, recv_sem=recv, device_id=device, device_id_type=MESH
    )


def build_band(taps_ref, band):
    rho = lax.broadcasted_iota(jnp.int32, (8, N), 0)
    lane = lax.broadcasted_iota(jnp.int32, (8, N), 1)
    shifted = 4 * lane - rho
    base = jnp.zeros((8, N), jnp.float32)
    for j in range(TAPS):
        base = jnp.where(shifted == j - 3, taps_ref[j], base)
    for t in range(BAND // 8):
        move = (2 * t - 32) % N
        tap = 4 * lane + (131 - 8 * t) - rho
        rolled = base if move == 0 else pltpu.roll(base, move, 1)
        band[8 * t : 8 * t + 8, :] = jnp.where((tap >= 0) & (tap < TAPS), rolled, 0.0)


def build_picker(index_ref):
    row = lax.broadcasted_iota(jnp.int32, (NSRC, 2 * GROUP), 0)
    wanted = jnp.zeros((NSRC, 2 * GROUP), jnp.int32)
    for s in range(NSRC):
        wanted = jnp.where(row == s, index_ref[s], wanted)
    owned = lax.broadcasted_iota(jnp.int32, (NSRC, 2 * GROUP), 1) % GROUP + lax.axis_index("chan") * GROUP
    return jnp.where(wanted == owned, 1.0, 0.0).astype(jnp.bfloat16)


def kernel(
    strain_hbm, taps_ref, index_ref, first_hbm, second_hbm, third_hbm, last_hbm, turn_hbm, win_hbm, out_hbm,
    raw, band, dec, pick, pick_in, total, rs_in, acc, row_buf, rows_in, halves, chan_in, src_all, spec_c, chan_op, spec, prod,
    first, second, third, last, turn, win,
    load_sem, own_sem, pick_sem, dec_send, dec_recv, rs_send, rs_recv, row_send, row_recv,
    g_send, g_recv, f_send, f_recv, out_sem,
):
    tm = lax.axis_index("tm")
    ch = lax.axis_index("chan")
    x, zh = tm % 4, tm // 4
    y, zl, core = ch // 4, (ch // 2) % 2, ch % 2
    z, pair = 2 * zh + zl, ch // 2

    tables = (
        (first_hbm, first), (second_hbm, second), (third_hbm, third), (last_hbm, last), (turn_hbm, turn),
        (win_hbm, win),
    )
    load = pltpu.make_async_copy(strain_hbm, raw.at[:, pl.ds(N, 4 * N * BLOCKS)], load_sem.at[0])
    load.start()
    loads = [pltpu.make_async_copy(a, b, load_sem.at[1 + i]) for i, (a, b) in enumerate(tables)]
    for copy in loads:
        copy.start()

    ring_x = [x] + [(x + d) % 4 for d in (1, 2, 3)]
    ring_y = [y] + [(y + d) % 4 for d in (1, 2, 3)]
    ring_z = [z] + [(z + d) % 4 for d in (1, 2, 3)]
    part_y = [16 * v for v in ring_y]
    part_z = [8 * (v % 2) + 4 * (v // 2) for v in ring_z]
    devices = {("x", d): (zh * 4 + ring_x[d], ch) for d in (1, 2, 3)}
    devices.update({("y", d): (tm, ring_y[d] * 4 + zl * 2 + core) for d in (1, 2, 3)})
    devices.update(
        {("z", d): ((ring_z[d] // 2) * 4 + x, y * 4 + (ring_z[d] % 2) * 2 + core) for d in (1, 2, 3)}
    )
    own_rows = core * HALF

    def device(axis, d):
        return devices[axis, d]

    sibling = (tm, 2 * pair + 1 - core)
    plane = 8 * zl + tm

    def in_plane(n):
        return (n % TM, 4 * y + 2 * (n // TM) + core)

    peers = [sibling]
    peers += [device("y", d) for d in ORDER]
    peers += [in_plane((plane + d) % 16) for d in range(1, 16)]
    barrier = pltpu.get_barrier_semaphore()
    for peer in peers:
        pl.semaphore_signal(barrier, inc=1, device_id=peer, device_id_type=MESH)

    raw[:, :N] = jnp.zeros((GROUP, N), jnp.float32)
    build_band(taps_ref, band)
    picker = build_picker(index_ref)
    b_hi, b_lo = split(band[...])
    both = jnp.concatenate([b_hi, b_lo], axis=1)
    load.wait()

    def finish(half, block, value):
        for j in range(TM):
            dec[j, half * HB + block] = value[8 * j : 8 * j + 8]
        picked = mm(picker, jnp.concatenate(split(value), axis=0))
        for j in range(NSRC // 8):
            pick[half, j, block] = picked[8 * j : 8 * j + 8]

    hi, lo = split(raw[:, 4 * N * BLOCKS :])
    wide = mm(hi, both[:N])
    finish(1, HB, wide[:, :N] + wide[:, N:] + mm(lo, b_hi[:N]))
    for j in range(NSRC // 8):
        pick[0, j, HB] = jnp.zeros((8, N), jnp.float32)

    def filter_half(half):
        for b0 in range(0, HB, 4):
            his, los = [], []
            for b in range(b0, b0 + 4):
                start = pl.multiple_of((half * HB + b) * (4 * N), 4 * N)
                hi, lo = split(raw[:, pl.ds(start, BAND)])
                his.append(hi)
                los.append(lo)
            hi, lo = jnp.concatenate(his, axis=0), jnp.concatenate(los, axis=0)
            wide = mm(hi, both)
            value = wide[:, :N] + wide[:, N:] + mm(lo, b_hi)
            for b in range(b0, b0 + 4):
                finish(half, b, value[GROUP * (b - b0) : GROUP * (b - b0 + 1)])

    started = []

    filter_half(1 - core)
    pl.semaphore_wait(barrier, len(peers))
    give = remote(pick.at[1 - core], pick_in, pick_sem.at[0], pick_sem.at[1], sibling)
    give.start()
    filter_half(core)
    own_blocks = pltpu.make_async_copy(dec.at[tm], chan_in.at[tm], own_sem.at[0])
    own_blocks.start()

    blocks = []
    for d in (1, 3, 2, 4, 5, 7, 6):
        other = (tm + d) % TM
        copy = remote(dec.at[other], chan_in.at[tm], dec_send.at[d], dec_recv.at[d], (other, ch))
        copy.start()
        blocks.append(copy)
    give.wait_recv()
    total[...] = pick[core] + pick_in[...]
    sums = []
    for d in ORDER:
        copy = remote(
            total.at[pl.ds(2 * ring_y[d], 2)], rs_in.at[d], rs_send.at[d], rs_recv.at[d], device("y", d)
        )
        copy.start()
        sums.append(copy)
    for copy in sums:
        copy.wait_recv()
    acc[...] = (total[pl.ds(2 * y, 2)] + rs_in[1] + rs_in[2] + rs_in[3]).reshape(2 * PART * 8, N)
    for n in range(16):
        row_buf[n, :PART] = acc[pl.ds((n // TM) * PART * 8 + n % TM, PART, stride=8), :]
        row_buf[n, PART:] = jnp.zeros((16 - PART, N), jnp.float32)
    rows = []
    for d in range(1, 16):
        other = (plane + d) % 16
        copy = remote(row_buf.at[other], rows_in.at[zl, tm], row_send.at[d], row_recv.at[d], in_plane(other))
        copy.start()
        rows.append(copy)
    rows_in[zl, tm] = row_buf[plane]
    for copy in loads:
        copy.wait()
    for copy in rows:
        copy.wait_recv()
    halves[core] = rows_in[0] + rows_in[1]
    swap = remote(halves.at[core], halves.at[core], pick_sem.at[2], pick_sem.at[3], sibling)
    swap.start()
    swap.wait_recv()
    place = lax.broadcasted_iota(jnp.int32, (HB, N), 0)
    pieces = []
    for j in range(TM):
        early = halves[0, j, :HB]
        if j > 0:
            early = early + jnp.where(place == 0, halves[1, j - 1, HB : HB + 1], 0.0)
        pieces += [early, halves[1, j, :HB]]
    src_all[0, 0, 0] = whiten_series([jnp.concatenate(pieces, axis=0)], first, second, third, last, turn)[0]

    REST = pl.ds(1, 3)

    def region(kind, offsets):
        start, size, order = KINDS[kind]
        at = dict(zip(order, offsets))
        return src_all.at[at["y"], at["z"], at["x"], pl.ds(own_rows + start, size)]

    counts = [{}, {}]

    def number(which, key):
        return counts[which].setdefault(key, len(counts[which]))

    def placed(offsets, axis, d):
        return tuple((4 - d) if i == axis else o for i, o in enumerate(offsets))

    def tag(offsets):
        return tuple("*" if not isinstance(o, int) else o for o in offsets)

    def send_on(kind, offsets, axis):
        for d in ORDER:
            to = placed(offsets, axis, d)
            n = number(0, (kind, tag(to), axis))
            copy = remote(
                region(kind, offsets), region(kind, to), g_send.at[n], g_recv.at[n], device(KINDS[kind][2][axis], d)
            )
            copy.start()
            started.append(copy)

    def arrived(kind, offsets, axis, ds=ORDER):
        for d in ds:
            to = placed(offsets, axis, d)
            n = number(0, (kind, tag(to), axis))
            part = region(kind, to)
            remote(part, part, g_send.at[n], g_recv.at[n], sibling).wait_recv()

    def share(kind, offsets):
        part = region(kind, offsets)
        n = number(1, (kind, tag(offsets)))
        copy = remote(part, part, f_send.at[n], f_recv.at[n], sibling)
        copy.start()
        started.append(copy)
        shared.append(copy)

    def settle():
        for copy in shared:
            copy.wait_recv()
        shared.clear()

    shared = []
    kinds = range(3)
    for axis in range(3):
        for kind in kinds:
            send_on(kind, (0, 0, 0), axis)

    place = lax.broadcasted_iota(jnp.int32, (BLOCKS, N), 0)

    def channel(c):
        pieces = []
        for j in range(TM):
            value = chan_in[j, :BLOCKS, c, :]
            if j > 0:
                value = value + jnp.where(place == 0, chan_in[j - 1, BLOCKS, c : c + 1, :], 0.0)
            pieces.append(value)
        return jnp.concatenate(pieces, axis=0)

    def channels(c0):
        whites = whiten_series([channel(c) for c in range(c0, c0 + 4)], first, second, third, last, turn)
        data = [jnp.concatenate([w, pltpu.roll(w, N - 1, 1)], axis=0) for w in whites]
        res = mm3((win[0], win[1]), split(jnp.concatenate(data, axis=1)))
        for i in range(2 * N // 8):
            for c in range(4):
                at = 8 * (c0 + c)
                spec_c[i, at : at + 8] = res[8 * i : 8 * i + 8, N * c : N * (c + 1)]

    def channel_slots(i, carry):
        for k in range(8):
            re = spec_c[i, pl.ds(k, 8, stride=8), :]
            im = spec_c[i + N // 8, pl.ds(k, 8, stride=8), :]
            straight, crossed = (re, im), (im, -re)
            if k == 0:
                single = jnp.broadcast_to(i == 0, re.shape)
                straight = (re, jnp.where(single, 0.0, im))
                crossed = (jnp.where(single, 0.0, im), jnp.where(single, im, -re))
            whole = []
            for halves in (straight, crossed):
                for r in range(-LAG_ROWS // 2, LAG_ROWS // 2):
                    moved = [h if r == 0 else pltpu.roll(h, -r % N, 1) for h in halves]
                    whole.append(jnp.concatenate(moved, axis=1))
            hi, lo = split(jnp.concatenate(whole, axis=0))
            chan_op[i * 8 + k] = jnp.concatenate([hi, lo], axis=0)
        return carry

    for kind in kinds:
        arrived(kind, (0, 0, 0), 0)
        send_on(kind, (REST, 0, 0), 1)
    for kind in kinds:
        arrived(kind, (0, 0, 0), 1)
        send_on(kind, (REST, 0, 0), 2)
        send_on(kind, (0, REST, 0), 2)
    for kind in kinds:
        arrived(kind, (0, 0, 0), 2)
        share(kind, (REST, 0, 0))
        share(kind, (0, REST, 0))
        share(kind, (0, 0, REST))
    own_blocks.wait()
    for copy in blocks:
        copy.wait_recv()
    channels(0)
    for kind in kinds:
        arrived(kind, (REST, 0, 0), 1)
        send_on(kind, (REST, REST, 0), 2)
    for kind in kinds:
        share(kind, (REST, REST, 0))
    channels(4)
    lax.fori_loop(0, N // 8, channel_slots, 0)
    for kind in kinds:
        arrived(kind, (REST, 0, 0), 2)
        share(kind, (REST, 0, REST))
        arrived(kind, (0, REST, 0), 2)
        share(kind, (0, REST, REST))
    settle()

    w_hi, w_lo = win[0][:, :N], win[1][:, :N]
    w_both = jnp.concatenate([w_hi, w_hi], axis=1)

    def transform(places):
        hi, lo = split(jnp.concatenate([src_all[ry, rz, rx] for ry, rz, rx in places], axis=1))
        rows = []
        for ry, rz, rx in places:
            source = part_y[ry] + part_z[rz] + ring_x[rx]
            rows.append(pl.ds(pl.multiple_of(source * 8, 8), 8))
        res = mm(w_both, jnp.concatenate([hi, lo], axis=0)) + mm(w_lo, hi)
        for i in range(2 * N // 8):
            for e, at in enumerate(rows):
                spec[i, at, :] = res[8 * i : 8 * i + 8, N * e : N * (e + 1)]

    def hand_over(d):
        for kind in kinds:
            arrived(kind, (REST, REST, 0), 2, (d,))
            share(kind, (REST, REST, 4 - d))

    near = [(ry, rz, 0) for ry in range(4) for rz in range(4)]
    near += [(ry, rz, rx) for ry, rz in ((0, 0), (1, 0), (2, 0), (3, 0), (0, 1), (0, 2), (0, 3)) for rx in (1, 2, 3)]
    transform(near[:8])
    transform(near[8:16])
    hand_over(1)
    hand_over(3)
    transform(near[16:23])
    transform(near[23:30])
    transform(near[30:])
    hand_over(2)
    settle()
    for ry in (1, 2, 3):
        transform([(ry, rz, rx) for rz in (1, 2, 3) for rx in (1, 2, 3)])

    left = lax.broadcasted_iota(jnp.int32, (NSRC, N), 1) < HALF

    def slots(i, carry):
        for k in range(UNROLL):
            n = i * UNROLL + k
            tile = i * (UNROLL // 8) + k // 8
            re = spec[tile, pl.ds(k % 8, NSRC, stride=8), :]
            im = spec[tile + N // 8, pl.ds(k % 8, NSRC, stride=8), :]
            hi, lo = split(jnp.concatenate([re, im], axis=1))
            res = lax.dot_general(
                chan_op[n],
                jnp.concatenate([hi, lo], axis=0),
                (((1,), (1,)), ((), ())),
                preferred_element_type=jnp.float32,
            )
            u = res[:64] + jnp.where(left, res[64:], 0.0)
            v = u + pltpu.roll(u, HALF, 1)
            prod[:, n] = jnp.where(left[:32], v[:32], v[32:]).reshape(LAG_ROWS, 8, N)
            if k % 32 == 31:
                part = pl.ds(i * UNROLL + k - 31, 32)
                sem = out_sem.at[i * (UNROLL // 32) + k // 32]
                pltpu.make_async_copy(prod.at[:, part], out_hbm.at[:, part], sem).start()
        return carry

    lax.fori_loop(0, N // UNROLL, slots, 0)

    for i in range(N // 32):
        part = pl.ds(i * 32, 32)
        pltpu.make_async_copy(prod.at[:, part], out_hbm.at[:, part], out_sem.at[i]).wait()
    swap.wait_send()
    give.wait_send()
    for copy in sums + rows + blocks + started:
        copy.wait_send()


def lags_kernel(prod_hbm, back_hbm, out_hbm, prod, back, out, in_sem, out_sem):
    table = pltpu.make_async_copy(back_hbm, back, in_sem.at[LAG_ROWS])
    table.start()
    loads = [pltpu.make_async_copy(prod_hbm.at[r], prod.at[r], in_sem.at[r]) for r in range(LAG_ROWS)]
    for copy in loads:
        copy.start()
    table.wait()
    k_hi = back[0]
    k_both = jnp.concatenate([back[0], back[1]], axis=1)
    for r in range(LAG_ROWS):
        loads[r].wait()
        for c0 in range(0, 8, 4):
            turned = [prod[r, :, c0 + c, :].T for c in range(4)]
            hi, lo = split(jnp.concatenate([jnp.concatenate([t[:NSRC], t[NSRC:]], axis=1) for t in turned], axis=0))
            wide = mm(hi, k_both)
            value = wide[:, :N] + wide[:, N:] + mm(lo, k_hi)
            out[c0 : c0 + 4, :, N * r : N * (r + 1)] = value.reshape(4, NSRC, N)
            if r == LAG_ROWS - 1:
                part = pl.ds(c0, 4)
                pltpu.make_async_copy(out.at[part], out_hbm.at[part], out_sem.at[c0 // 4]).start()
    for c0 in range(0, 8, 4):
        part = pl.ds(c0, 4)
        pltpu.make_async_copy(out.at[part], out_hbm.at[part], out_sem.at[c0 // 4]).wait()


def on_device(strain, fir_taps, source_index):
    tables = series_tables()
    win, back = window_tables()
    tables = [stack_np(t) for t in tables[:4]] + [tables[4], stack_np(win)]
    dma = pltpu.SemaphoreType.DMA
    f32 = jnp.float32
    smem = pl.BlockSpec(memory_space=pltpu.SMEM)
    anywhere = pl.BlockSpec(memory_space=pl.ANY)
    products = pl.pallas_call(
        kernel,
        out_shape=jax.ShapeDtypeStruct((LAG_ROWS, N, 8, N), f32),
        in_specs=[anywhere, smem, smem] + [anywhere] * len(tables),
        out_specs=anywhere,
        scratch_shapes=[
            VMEM((GROUP, N + 4 * N * BLOCKS), f32),
            VMEM((BAND, N), f32),
            VMEM((TM, BLOCKS + 1, 8, N), f32),
            VMEM((2, 8, PART, 8, N), f32),
            VMEM((8, PART, 8, N), f32),
            VMEM((8, PART, 8, N), f32),
            VMEM((4, 2, PART, 8, N), f32),
            VMEM((2 * PART * 8, N), f32),
            VMEM((16, 16, N), f32),
            VMEM((2, TM, 16, N), f32),
            VMEM((2, TM, 16, N), f32),
            VMEM((TM, BLOCKS + 1, 8, N), f32),
            VMEM((4, 4, 4, N, N), f32),
            VMEM((2 * N // 8, 64, N), f32),
            VMEM((N, N, 2 * N), jnp.bfloat16),
            VMEM((2 * N // 8, 8 * NSRC, N), f32),
            VMEM((LAG_ROWS, N, 8, N), f32),
        ]
        + [VMEM(t.shape, jnp.dtype(t.dtype)) for t in tables]
        + [
            dma((1 + len(tables),)),
            dma((2,)),
            dma((4,)),
            dma((TM,)),
            dma((TM,)),
            dma((4,)),
            dma((4,)),
            dma((16,)),
            dma((16,)),
        ]
        + [dma((81,))] * 2
        + [dma((27,))] * 2
        + [dma((N // 32,))],
        compiler_params=pltpu.CompilerParams(
            collective_id=0, has_side_effects=True, vmem_limit_bytes=VMEM_LIMIT
        ),
        name="interferometry",
    )(strain, fir_taps, source_index, *tables)
    return pl.pallas_call(
        lags_kernel,
        out_shape=jax.ShapeDtypeStruct((8, NSRC, LAG_ROWS * N), f32),
        in_specs=[anywhere, anywhere],
        out_specs=anywhere,
        scratch_shapes=[
            VMEM((LAG_ROWS, N, 8, N), f32),
            VMEM((2, 2 * N, N), jnp.bfloat16),
            VMEM((8, NSRC, LAG_ROWS * N), f32),
            dma((LAG_ROWS + 1,)),
            dma((2,)),
        ],
        compiler_params=pltpu.CompilerParams(vmem_limit_bytes=VMEM_LIMIT),
        name="lags",
    )(products, stack_np(back))


def solution(mesh):
    return jax.shard_map(
        on_device,
        mesh=mesh,
        in_specs=(P("chan", "tm"), P(), P()),
        out_specs=P(("chan", "tm"), None, None),
        check_vma=False,
    )
```
